32 devices in a mesh: var: 4 (over z), dp: 2 (over core), segment: 4 (over y, x).
Axes of the slice: x: 2, y: 2, z: 4, core: 2. Of those that a mesh axis runs over, the one named last changes fastest.
Arguments:
- queries: bfloat16 [2, 4, 4, 256, 1024], P('dp', 'segment', 'var'), parts along dimension 0, may hold values from -22 to 22
- keys: bfloat16 [2, 4, 4, 256, 1024], P('dp', 'segment', 'var'), parts along dimension 0, may hold values from -22 to 22
- values: bfloat16 [2, 4, 4, 256, 1024], P('dp', 'segment', 'var'), parts along dimension 0, may hold values from -6 to 6
- out_grad: bfloat16 [2, 4, 4, 256, 1024], P('dp', 'segment', 'var'), parts along dimension 0, may hold values from -96 to 96
- proj_weight: bfloat16 [4, 2048, 3072], P('segment', 'var'), may hold values from -0.125 to 0.125
- links: int32 [4, 3], replicated, may hold values from -1 to 3, as said below
Outputs:
- passed: bfloat16 [2, 4, 4, 256, 2048], P('dp', 'segment', 'var'), parts along dimension 0
The draws below stay inside these ranges and needn't reach their ends.
There are 2 independent parts, one for each index of `dp`. The reference program is written for one: setup_inputs(seed, part) draws one part's arguments, and reference() takes and returns one part's arrays. A program takes and returns all parts, laid end to end along the dimension named above; an argument that names none is the same for every part. Nothing has to cross between parts.
Inputs may be any that keep to these rules, and one draw needn't show every extreme that they name: `links`: row v lists v itself and some of the 2 variables at cyclic distance 1 to 1 from v (indices modulo 4), each at most once, listed first in order of signed offset, the remaining entries -1; some variable lists all 3.
All inputs are finite; a program needn't handle non-finite values.
Results may differ from the reference program's by a relative error of at most 0.007.
Values may be sent and summed in bfloat16 or wider, within the bound.
No kernel may reach another device: no remote copies, remote signals or barrier semaphores. Data moves between devices by JAX's collectives and lax.ppermute only.
A program may use at most 256 MiB of HBM per device.

```python
import math
import jax
import jax.numpy as jnp
from jax import lax

D = 2048
HEADS = 16
HS = 64
PATCHES = 256
CAUSAL_BLOCK = 128
HD = 1024
VARS = 4
SEGMENTS = 4
REACH = 1


def drawn_pair(key, part):
    root_random_key = jax.random.fold_in(key, 11)
    query_random_key, random_key_for_keys = jax.random.split(root_random_key, 2)
    full_shape = (1, SEGMENTS, VARS, PATCHES, HEADS, HS)
    query_draw = jnp.clip(jax.random.normal(query_random_key, full_shape, jnp.float32), -4.0, 4.0)
    key_draw = jnp.clip(jax.random.normal(random_key_for_keys, full_shape, jnp.float32), -4.0, 4.0)
    flat_shape = (1, SEGMENTS, VARS, PATCHES, HEADS * HS)
    return (query_draw.reshape(flat_shape), key_draw.reshape(flat_shape))


def draw_queries(key, part):
    return drawn_pair(key, part)[0].astype(jnp.bfloat16)


def draw_keys(key, part):
    return drawn_pair(key, part)[1].astype(jnp.bfloat16)


def draw_links(key, part):
    root_random_key = jax.random.fold_in(key, 5)
    key_present, key_full = jax.random.split(root_random_key, 2)
    window = 2 * REACH + 1
    offsets = jnp.arange(window, dtype=jnp.int32) - REACH
    present = jax.random.randint(key_present, (VARS, window), 0, 2)
    present = jnp.where(offsets[None, :] == 0, 1, present)
    full_row = jax.random.randint(key_full, (), 0, VARS)
    present = jnp.where(jnp.arange(VARS)[:, None] == full_row, 1, present)
    neighbor_ids = (jnp.arange(VARS, dtype=jnp.int32)[:, None] + offsets[None, :]) % VARS
    neighbor_ids = jnp.where(present == 1, neighbor_ids, -1)
    order = jnp.argsort(1 - present, axis=1, stable=True)
    return jnp.take_along_axis(neighbor_ids, order, axis=1).astype(jnp.int32)


def levels(own_key, dims, cuts, least, high):
    level = 1.0
    for axis_at, blocks in cuts:
        heights = jax.random.uniform(jax.random.fold_in(jax.random.fold_in(own_key, 6), axis_at), (blocks,), jnp.float32, least / len(cuts), high / len(cuts))
        level = level * jnp.repeat(jnp.exp(heights), dims[axis_at] // blocks).reshape((-1,) + (1,) * (len(dims) - 1 - axis_at))
    return level


def scatter_about(key, shape, scale, bound, cuts=(), kind=jnp.bfloat16):
    level = levels(key, shape, cuts, -0.22, 0.18) if cuts else 1.0
    result = jax.random.normal(key, shape, jnp.float32) * scale * level
    return jnp.minimum(jnp.maximum(result, -bound), bound).astype(kind)


def setup_inputs(seed: int = 0, part: int = 0) -> dict:
    arg_keys = jax.random.split(jax.random.key(seed), 7)
    part_keys = jax.random.split(jax.random.fold_in(arg_keys[6], part), 7)
    return {
        "queries": draw_queries(jax.random.fold_in(jax.random.fold_in(arg_keys[6], part), 71), part),
        "keys": draw_keys(jax.random.fold_in(jax.random.fold_in(arg_keys[6], part), 71), part),
        "values": scatter_about(part_keys[2], (1, SEGMENTS, VARS, PATCHES, HD), 1.0, 6.0, ((1, 4), (2, 4))),
        "out_grad": scatter_about(part_keys[3], (1, SEGMENTS, VARS, PATCHES, HD), 16.0, 96.0, ((1, 4), (2, 4))),
        "proj_weight": scatter_about(arg_keys[4], (SEGMENTS, D, 3 * HD), D ** -0.5, 0.125, ((0, 4), (1, 4))),
        "links": draw_links(jax.random.fold_in(arg_keys[6], 71), part),
    }


neg_big = -1e+30

def segment_grads(query_all, key_all, value_all, grad_all, weight, links):
    var_count, patches, feature_width = query_all.shape
    head_size = feature_width // HEADS
    score_scale = 1.0 / math.sqrt(head_size)
    token_shape = (var_count, patches, HEADS, head_size)
    query_heads = query_all.reshape(token_shape).astype(jnp.float32)
    key_heads = key_all.reshape(token_shape).astype(jnp.float32)
    value_heads = value_all.reshape(token_shape).astype(jnp.float32)
    grad_heads = grad_all.reshape(token_shape).astype(jnp.float32)
    offsets = jnp.arange(2 * REACH + 1, dtype=jnp.int32) - REACH
    block_index = jnp.arange(patches, dtype=jnp.int32) // CAUSAL_BLOCK
    causal = block_index[:, None] >= block_index[None, :]

    def one_var(carry, variable):
        key_acc, value_acc = carry
        window_ids = ((variable + offsets) % var_count).astype(jnp.int32)
        own_links = lax.dynamic_index_in_dim(links, variable, 0, keepdims=False)
        linked = jnp.any(own_links[None, :] == window_ids[:, None], axis=1)
        key_block = key_heads[window_ids]
        value_block = value_heads[window_ids]
        own_query = lax.dynamic_index_in_dim(query_heads, variable, 0, keepdims=False)
        own_grad = lax.dynamic_index_in_dim(grad_heads, variable, 0, keepdims=False)
        scores = jnp.einsum('phe,wqhe->hpwq', own_query, key_block) * score_scale
        allowed = linked[None, None, :, None] & causal[None, :, None, :]
        scores = jnp.where(allowed, scores, neg_big)
        grad_attn = jnp.einsum('phe,wqhe->hpwq', own_grad, value_block)
        row_max = scores.max(axis=(2, 3), keepdims=True)
        log_total = row_max + jnp.log(jnp.exp(scores - row_max).sum(axis=(2, 3), keepdims=True))
        attention = jnp.exp(scores - log_total)
        row_delta = (attention * grad_attn).sum(axis=(2, 3), keepdims=True)
        attention_low = lax.optimization_barrier(attention.astype(jnp.bfloat16)).astype(jnp.float32)
        score_grad = lax.optimization_barrier((score_scale * attention * (grad_attn - row_delta)).astype(jnp.bfloat16)).astype(jnp.float32)
        grad_query = jnp.einsum('hpwq,wqhe->phe', score_grad, key_block).astype(jnp.bfloat16)
        key_part = jnp.einsum('hpwq,phe->wqhe', score_grad, own_query).astype(jnp.bfloat16)
        value_part = jnp.einsum('hpwq,phe->wqhe', attention_low, own_grad).astype(jnp.bfloat16)
        key_acc = key_acc.at[window_ids].add(key_part.astype(jnp.float32))
        value_acc = value_acc.at[window_ids].add(value_part.astype(jnp.float32))
        return ((key_acc, value_acc), grad_query)
    zeros = jnp.zeros(token_shape, jnp.float32)
    (key_grad, value_grad), query_grad = lax.scan(one_var, (zeros, zeros), jnp.arange(var_count, dtype=jnp.int32))
    flat_shape = (var_count, patches, feature_width)
    qkv_grad = jnp.concatenate([query_grad.reshape(flat_shape), key_grad.astype(jnp.bfloat16).reshape(flat_shape), value_grad.astype(jnp.bfloat16).reshape(flat_shape)], axis=2)
    input_grad = jnp.dot(qkv_grad.reshape(var_count * patches, 3 * feature_width), weight.T, preferred_element_type=jnp.float32)
    return input_grad.astype(jnp.bfloat16).reshape(var_count, patches, weight.shape[0])

def reference(queries, keys, values, out_grad, proj_weight, links):

    def per_segment(segment_args):
        query_all, key_all, value_all, grad_all, weight = segment_args
        return segment_grads(query_all, key_all, value_all, grad_all, weight, links)
    input_grad = lax.map(per_segment, (queries[0], keys[0], values[0], out_grad[0], proj_weight))
    passed = jnp.concatenate([input_grad[1:], input_grad[:1]], axis=0)
    return passed[None]
```

```python
import functools
import math

import jax
import jax.numpy as jnp
from jax import lax
from jax.experimental import pallas as pl
from jax.experimental.pallas import tpu as pltpu
from jax.sharding import PartitionSpec as P

HEADS = 16
CAUSAL_BLOCK = 128
GROUP = 4

neg_big = -1e30
f32 = jnp.float32
bf16 = jnp.bfloat16


def passed_along(block, axis, distance):
    devices = range(lax.axis_size(axis))
    route = [((i - distance) % len(devices), i) for i in devices]
    return lax.ppermute(block, axis, route)


def after(block, *earlier):
    return lax.optimization_barrier((block,) + earlier)[0]


def dot_nt(a, b):
    return lax.dot_general(a, b, (((1,), (1,)), ((), ())), preferred_element_type=f32)


def dot_nn(a, b):
    return lax.dot_general(a, b, (((1,), (0,)), ((), ())), preferred_element_type=f32)


def own_half(block, half, head_size):
    lane = lax.broadcasted_iota(jnp.int32, block.shape, 1)
    keep = (lane < head_size) if half == 0 else (lane >= head_size)
    return jnp.where(keep, block, jnp.zeros_like(block))


def block_products(key_half, value_half, query, grad, blocks):
    out = []
    for j in range(blocks):
        rows = slice(j * CAUSAL_BLOCK, (j + 1) * CAUSAL_BLOCK)
        start = j * CAUSAL_BLOCK
        out.append(
            (dot_nt(key_half[rows], query[start:]), dot_nt(value_half[rows], grad[start:]))
        )
    return out


def stats_kernel(sources, head_size, scale, linked_ref, k_ref, v_ref, *refs):
    ins, outs = refs[: 2 * sources], refs[2 * sources :]
    patches = k_ref.shape[0]
    blocks = patches // CAUSAL_BLOCK
    factor = scale * math.log2(math.e)
    for s in range(sources):
        linked = linked_ref[s] != 0
        lams, deltas = [], []
        for h in range(GROUP):
            cols = slice((h // 2) * 2 * head_size, (h // 2 + 1) * 2 * head_size)
            key_half = own_half(k_ref[:, cols], h % 2, head_size)
            value_half = own_half(v_ref[:, cols], h % 2, head_size)
            parts = block_products(
                key_half, value_half, ins[2 * s][:, cols], ins[2 * s + 1][:, cols], blocks
            )
            lam_row, delta_row = [], []
            for i in range(blocks):
                pieces = []
                for j in range(i + 1):
                    at = slice((i - j) * CAUSAL_BLOCK, (i - j + 1) * CAUSAL_BLOCK)
                    pieces.append((parts[j][0][:, at], parts[j][1][:, at]))
                top = functools.reduce(
                    jnp.maximum, [jnp.max(p[0], axis=0, keepdims=True) for p in pieces]
                )
                total = 0.0
                weighted = 0.0
                for score, grad_attn in pieces:
                    e = jnp.exp2((score - top) * factor)
                    total = total + jnp.sum(e, axis=0, keepdims=True)
                    weighted = weighted + jnp.sum(e * grad_attn, axis=0, keepdims=True)
                lam_row.append(top + jnp.log(total) * (1.0 / scale))
                delta_row.append(weighted / total)
            lams.append(jnp.concatenate(lam_row, axis=1))
            deltas.append(jnp.concatenate(delta_row, axis=1))
        lam = jnp.where(linked, jnp.concatenate(lams, axis=0), neg_big)
        delta = jnp.where(linked, jnp.concatenate(deltas, axis=0), 0.0)
        outs[s][0] = jnp.concatenate([lam, delta], axis=0)


def grads_kernel(sources, window, head_size, scale, linked_ref, k_ref, v_ref, *refs):
    ins = refs[: 2 * sources]
    stats = refs[2 * sources : 2 * sources + sources * window]
    outs = refs[2 * sources + sources * window :]
    own_out, part_outs, kv_out = outs[0], outs[1:sources], outs[sources]
    patches = k_ref.shape[0]
    blocks = patches // CAUSAL_BLOCK
    factor = scale * math.log2(math.e)
    key_t = jnp.transpose(k_ref[...].astype(f32)).astype(bf16)
    totals = []
    for s in range(sources):
        lams = [r[0, :GROUP] for r in stats[s * window : (s + 1) * window]]
        deltas = [r[0, GROUP:] for r in stats[s * window : (s + 1) * window]]
        top = functools.reduce(jnp.maximum, lams)
        weights = [jnp.exp2((lam - top) * factor) for lam in lams]
        total = functools.reduce(jnp.add, weights)
        delta = functools.reduce(jnp.add, [w * d for w, d in zip(weights, deltas)]) / total
        lam = top + jnp.log(total) * (1.0 / scale)
        lam = jnp.where(linked_ref[s] != 0, lam, -neg_big)
        totals.append((lam, delta))
    for pair in range(GROUP // 2):
        cols = slice(pair * 2 * head_size, (pair + 1) * 2 * head_size)
        halves = [
            (
                own_half(k_ref[:, cols], half, head_size),
                own_half(v_ref[:, cols], half, head_size),
            )
            for half in range(2)
        ]
        key_sum = jnp.zeros((patches, 2 * head_size), f32)
        value_sum = jnp.zeros((patches, 2 * head_size), f32)
        for s in range(sources):
            query, grad = ins[2 * s][:, cols], ins[2 * s + 1][:, cols]
            query_t = []
            for half in range(2):
                h = 2 * pair + half
                lam = totals[s][0][h : h + 1]
                delta = totals[s][1][h : h + 1]
                parts = block_products(*halves[half], query, grad, blocks)
                attn_rows, score_rows = [], []
                for j in range(blocks):
                    start = j * CAUSAL_BLOCK
                    attn = jnp.exp2((parts[j][0] - lam[:, start:]) * factor)
                    score_grad = (attn * (parts[j][1] - delta[:, start:])).astype(bf16)
                    attn = attn.astype(bf16)
                    if start:
                        pad = jnp.zeros((CAUSAL_BLOCK, start), bf16)
                        attn = jnp.concatenate([pad, attn], axis=1)
                        score_grad = jnp.concatenate([pad, score_grad], axis=1)
                    attn_rows.append(attn)
                    score_rows.append(score_grad)
                attn = jnp.concatenate(attn_rows, axis=0)
                score_grad = jnp.concatenate(score_rows, axis=0)
                key_sum = key_sum + dot_nn(score_grad, own_half(query, half, head_size))
                value_sum = value_sum + dot_nn(attn, own_half(grad, half, head_size))
                query_t.append(dot_nn(key_t[h * head_size : (h + 1) * head_size], score_grad))
            part = jnp.transpose(jnp.concatenate(query_t, axis=0)) * scale
            if s == 0:
                own_out[:, cols] = part
            else:
                part_outs[s - 1][:, cols] = part.astype(bf16)
        kv_out[0, :, cols] = (key_sum * scale).astype(bf16)
        kv_out[1, :, cols] = value_sum.astype(bf16)


def specs(patches, width):
    token = pl.BlockSpec((patches, width), lambda g: (0, g))
    stat = pl.BlockSpec((1, 2 * GROUP, patches), lambda g: (g, 0, 0))
    flag = pl.BlockSpec(memory_space=pltpu.SMEM)
    return token, stat, flag


def block_stats(linked, keys, values, pairs, head_size, scale):
    patches, features = keys.shape
    token, stat, flag = specs(patches, GROUP * head_size)
    groups = HEADS // GROUP
    n = len(pairs)
    return pl.pallas_call(
        functools.partial(stats_kernel, n, head_size, scale),
        grid=(groups,),
        in_specs=[flag] + [token] * (2 + 2 * n),
        out_specs=[stat] * n,
        out_shape=[jax.ShapeDtypeStruct((groups, 2 * GROUP, patches), f32)] * n,
        compiler_params=pltpu.CompilerParams(vmem_limit_bytes=48 * 2**20),
        cost_estimate=pl.CostEstimate(
            flops=8 * n * patches * patches * features,
            bytes_accessed=4 * (n + 1) * patches * features,
            transcendentals=n * HEADS * patches * patches,
        ),
        name="row_stats",
    )(linked, keys, values, *[x for pair in pairs for x in pair])


def block_grads(linked, keys, values, pairs, stats, head_size, scale):
    patches, features = keys.shape
    token, stat, flag = specs(patches, GROUP * head_size)
    groups = HEADS // GROUP
    n = len(pairs)
    window = len(stats[0])
    both = pl.BlockSpec((2, patches, GROUP * head_size), lambda g: (0, 0, g))
    shape = jax.ShapeDtypeStruct
    return pl.pallas_call(
        functools.partial(grads_kernel, n, window, head_size, scale),
        grid=(groups,),
        in_specs=[flag] + [token] * (2 + 2 * n) + [stat] * (n * window),
        out_specs=[token] * n + [both],
        out_shape=[shape((patches, features), f32)]
        + [shape((patches, features), bf16)] * (n - 1)
        + [shape((2, patches, features), bf16)],
        compiler_params=pltpu.CompilerParams(vmem_limit_bytes=48 * 2**20),
        cost_estimate=pl.CostEstimate(
            flops=20 * n * patches * patches * features,
            bytes_accessed=8 * (n + 1) * patches * features,
            transcendentals=n * HEADS * patches * patches,
        ),
        name="block_grads",
    )(
        linked,
        keys,
        values,
        *[x for pair in pairs for x in pair],
        *[x for group in stats for x in group],
    )


def place_kernel(at_ref, *refs):
    out_ref = refs[-1]
    for i, ref in enumerate(refs[:-1]):
        width = ref.shape[1]
        col = pl.multiple_of(at_ref[i] * width, width)
        out_ref[pl.ds(0, ref.shape[0]), pl.ds(col, width)] = ref[...]


def times(tokens, rows):
    return dot_nt(tokens, rows).astype(bf16)


def swapped(block):
    return lax.ppermute(block, "dp", [(0, 1), (1, 0)])


def handed_on(result, patches, segments, outer=None):
    axes = ("dp", "segment") if outer is None else ("var", "dp", "segment")
    out = []
    for cross in range(2):
        route = []
        for src, dst in outer or [(0, 0)]:
            for d in range(2):
                for s in range(segments):
                    route.append(
                        (
                            (src * 2 + d) * segments + s,
                            (dst * 2 + (d + cross) % 2) * segments + (s - 1) % segments,
                        )
                    )
        out.append(
            lax.ppermute(result[cross * patches : (cross + 1) * patches], axes, route)
        )
    return out


def attention_grads(queries, keys, values, out_grad, links, reach, first, second, third):
    patches, feature_width = queries.shape
    head_size = feature_width // HEADS
    scale = 1.0 / math.sqrt(head_size)
    n = lax.axis_size("var")
    own = lax.axis_index("var")
    offsets = [0] + [o for d in range(1, reach + 1) for o in (d, -d)]
    pairs = [(queries, out_grad)]
    for o in offsets[1:]:
        pairs.append((passed_along(queries, "var", -o), passed_along(out_grad, "var", -o)))
    sources = (own + jnp.array(offsets, jnp.int32)) % n
    linked = jnp.any(links[sources] == own, axis=1).astype(jnp.int32)
    own_stats = block_stats(linked[:1], keys, values, pairs[:1], head_size, scale)
    first(own_stats[0])
    other_stats = block_stats(linked[1:], keys, values, pairs[1:], head_size, scale)
    stats = dict(zip(offsets, list(own_stats) + list(other_stats)))
    needed = {}
    for d in offsets:
        for e in offsets:
            entries = needed.setdefault((d + e) % n, [])
            if -e not in entries:
                entries.append(-e)
    arrived = {}
    for t, entries in needed.items():
        if t == 0:
            arrived[t] = {o: stats[o] for o in entries}
            continue
        entries.sort()
        message = jnp.stack([stats[o] for o in entries])
        message = passed_along(message, "var", -t)
        arrived[t] = {o: message[i] for i, o in enumerate(entries)}
    second(other_stats[0])
    windows = [[arrived[(d + e) % n][-e] for e in offsets] for d in offsets]
    grads = block_grads(linked, keys, values, pairs, windows, head_size, scale)
    third(grads[-1])
    query_grad = grads[0]
    for o, part in zip(offsets[1:], grads[1:-1]):
        query_grad = query_grad + passed_along(part, "var", o).astype(f32)
    return query_grad.astype(bf16), grads[-1]


def shards(queries, keys, values, out_grad, proj_weight, links):
    patches, feature_width = queries.shape[3:]
    n = lax.axis_size("var")
    segments = lax.axis_size("segment")
    reach = min(4, (n - 1) // 2)
    flat = [x.reshape(patches, feature_width) for x in (queries, keys, values, out_grad)]
    weight = proj_weight[0]
    if n != 4:
        nothing = lambda value: None
        query_grad, pair = attention_grads(*flat, links, reach, nothing, nothing, nothing)
        grad_qkv = jnp.concatenate([query_grad, pair[0], pair[1]], axis=1)
        whole = lax.all_gather(weight, "var", axis=0, tiled=True)
        passed = passed_along(times(grad_qkv, whole), "segment", -1)
        return passed.reshape(1, 1, 1, patches, whole.shape[0])

    own = lax.axis_index("var")
    core = lax.axis_index("dp")
    half = weight.shape[0] // 2
    cuts = [(0, half // 4), (half // 4, half * 5 // 8), (half * 5 // 8, half)]
    below, above = [], []

    def near(i):
        def start(value):
            lo, hi = cuts[i]
            piece = lax.dynamic_slice_in_dim(weight, core * half + lo, hi - lo, 0)
            piece = after(piece, value)
            below.append(lax.ppermute(piece, "var", [(0, 1), (1, 2), (2, 3)]))
            above.append(lax.ppermute(piece, "var", [(1, 0), (2, 1), (3, 2)]))

        return start

    query_grad, pair = attention_grads(*flat, links, reach, near(0), near(1), near(2))
    far = []
    for up, down in zip(below, above):
        up = lax.ppermute(after(up, pair), "var", [(1, 2), (2, 3)])
        down = lax.ppermute(after(down, pair), "var", [(1, 0), (2, 1)])
        far.append(jnp.where(own < 2, down, up))
    inward = [(0, 1), (3, 2)]
    outer_pair = lax.ppermute(pair, "var", inward)
    outer_query = lax.ppermute(query_grad, "var", inward)

    def tokens(query_part, pair_part):
        other_pair, other_query = swapped(pair_part), swapped(query_part)
        return jnp.concatenate(
            [
                jnp.concatenate([query_part, pair_part[0], pair_part[1]], axis=1),
                jnp.concatenate([other_query, other_pair[0], other_pair[1]], axis=1),
            ],
            axis=0,
        )

    own_tokens = tokens(query_grad, pair)
    outer_tokens = tokens(outer_query, outer_pair)
    own_rows = lax.dynamic_slice_in_dim(weight, core * half, half, 0)
    near_rows = jnp.concatenate([own_rows] + above + below, axis=0)
    handed = handed_on(times(own_tokens, near_rows), patches, segments)
    far_rows = jnp.concatenate(far, axis=0)
    handed_far = handed_on(times(own_tokens, far_rows), patches, segments)
    handed_end = handed_on(
        times(outer_tokens, far_rows), patches, segments, outer=[(1, 0), (2, 3)]
    )
    pieces, places = [], []
    for cross in range(2):
        side = (core + cross) % 2
        by_step = [handed[cross][:, i * half : (i + 1) * half] for i in range(3)]
        end = handed_end[cross]
        by_step = [
            by_step[0],
            jnp.where(own == 3, end, by_step[1]),
            handed_far[cross],
            jnp.where(own == 0, end, by_step[2]),
        ]
        for step, piece in enumerate(by_step):
            pieces.append(piece)
            places.append((own + step) % 4 * 2 + side)
    passed = pl.pallas_call(
        place_kernel,
        in_specs=[pl.BlockSpec(memory_space=pltpu.SMEM)]
        + [pl.BlockSpec(memory_space=pltpu.VMEM)] * 8,
        out_specs=pl.BlockSpec(memory_space=pltpu.VMEM),
        out_shape=jax.ShapeDtypeStruct((patches, 8 * half), bf16),
        name="placed",
    )(jnp.stack(places).astype(jnp.int32), *pieces)
    return passed.reshape(1, 1, 1, patches, 8 * half)


def solution(mesh):
    return jax.shard_map(
        shards,
        mesh=mesh,
        in_specs=(
            P("dp", "segment", "var", None, None),
            P("dp", "segment", "var", None, None),
            P("dp", "segment", "var", None, None),
            P("dp", "segment", "var", None, None),
            P("segment", "var", None),
            P(),
        ),
        out_specs=P("dp", "segment", "var", None, None),
        check_vma=False,
    )
```

```python
import functools
import math

import jax
import jax.numpy as jnp
from jax import lax
from jax.experimental import pallas as pl
from jax.experimental.pallas import tpu as pltpu
from jax.sharding import PartitionSpec as P

OPT = {'k1': 1, 'k2': 1, 'kp': 1, 'wa': 'first', 'st': 1, 'dq': 1, 'cb': 0, 'cuts': [128], 'nc': 'token', 'far': {0: 'lret', 1: 'lret', 2: 'lret'}, 'order': '', 'op': 'ret1', 'sf': 'rfpq', 'one': 1, 's1': '', 'ft': ['ret1', 'ret1']}

HEADS = 16
CAUSAL_BLOCK = 128
GROUP = 4

neg_big = -1e30
f32 = jnp.float32
bf16 = jnp.bfloat16


def passed_along(block, axis, distance):
    devices = range(lax.axis_size(axis))
    route = [((i - distance) % len(devices), i) for i in devices]
    return lax.ppermute(block, axis, route)


def spent(us):
    return pl.CostEstimate(flops=int(us * 1.15e9), bytes_accessed=1024, transcendentals=0)


def after(block, *earlier):
    return lax.optimization_barrier((block,) + earlier)[0]


def dot_nt(a, b):
    return lax.dot_general(a, b, (((1,), (1,)), ((), ())), preferred_element_type=f32)


def dot_nn(a, b):
    return lax.dot_general(a, b, (((1,), (0,)), ((), ())), preferred_element_type=f32)


def own_half(block, half, head_size):
    lane = lax.broadcasted_iota(jnp.int32, block.shape, 1)
    keep = (lane < head_size) if half == 0 else (lane >= head_size)
    return jnp.where(keep, block, jnp.zeros_like(block))


def block_products(key_half, value_half, query, grad, blocks):
    out = []
    for j in range(blocks):
        rows = slice(j * CAUSAL_BLOCK, (j + 1) * CAUSAL_BLOCK)
        start = j * CAUSAL_BLOCK
        out.append(
            (dot_nt(key_half[rows], query[start:]), dot_nt(value_half[rows], grad[start:]))
        )
    return out


def stats_kernel(sources, head_size, scale, linked_ref, k_ref, v_ref, *refs):
    ins, outs = refs[: 2 * sources], refs[2 * sources :]
    patches = k_ref.shape[0]
    blocks = patches // CAUSAL_BLOCK
    factor = scale * math.log2(math.e)
    for s in range(sources):
        linked = linked_ref[s] != 0
        lams, deltas = [], []
        for h in range(GROUP):
            cols = slice((h // 2) * 2 * head_size, (h // 2 + 1) * 2 * head_size)
            key_half = own_half(k_ref[:, cols], h % 2, head_size)
            value_half = own_half(v_ref[:, cols], h % 2, head_size)
            parts = block_products(
                key_half, value_half, ins[2 * s][:, cols], ins[2 * s + 1][:, cols], blocks
            )
            lam_row, delta_row = [], []
            for i in range(blocks):
                pieces = []
                for j in range(i + 1):
                    at = slice((i - j) * CAUSAL_BLOCK, (i - j + 1) * CAUSAL_BLOCK)
                    pieces.append((parts[j][0][:, at], parts[j][1][:, at]))
                top = functools.reduce(
                    jnp.maximum, [jnp.max(p[0], axis=0, keepdims=True) for p in pieces]
                )
                total = 0.0
                weighted = 0.0
                for score, grad_attn in pieces:
                    e = jnp.exp2((score - top) * factor)
                    total = total + jnp.sum(e, axis=0, keepdims=True)
                    weighted = weighted + jnp.sum(e * grad_attn, axis=0, keepdims=True)
                lam_row.append(top + jnp.log(total) * (1.0 / scale))
                delta_row.append(weighted / total)
            lams.append(jnp.concatenate(lam_row, axis=1))
            deltas.append(jnp.concatenate(delta_row, axis=1))
        lam = jnp.where(linked, jnp.concatenate(lams, axis=0), neg_big)
        delta = jnp.where(linked, jnp.concatenate(deltas, axis=0), 0.0)
        outs[s][0] = jnp.concatenate([lam, delta], axis=0)


def grads_kernel(sources, window, head_size, scale, linked_ref, k_ref, v_ref, *refs):
    ins = refs[: 2 * sources]
    stats = refs[2 * sources : 2 * sources + sources * window]
    outs = refs[2 * sources + sources * window :]
    own_out, part_outs, kv_out = outs[0], outs[1:sources], outs[sources]
    patches = k_ref.shape[0]
    blocks = patches // CAUSAL_BLOCK
    factor = scale * math.log2(math.e)
    key_t = jnp.transpose(k_ref[...].astype(f32)).astype(bf16)
    totals = []
    for s in range(sources):
        lams = [r[0, :GROUP] for r in stats[s * window : (s + 1) * window]]
        deltas = [r[0, GROUP:] for r in stats[s * window : (s + 1) * window]]
        top = functools.reduce(jnp.maximum, lams)
        weights = [jnp.exp2((lam - top) * factor) for lam in lams]
        total = functools.reduce(jnp.add, weights)
        delta = functools.reduce(jnp.add, [w * d for w, d in zip(weights, deltas)]) / total
        lam = top + jnp.log(total) * (1.0 / scale)
        lam = jnp.where(linked_ref[s] != 0, lam, -neg_big)
        totals.append((lam, delta))
    for pair in range(GROUP // 2):
        cols = slice(pair * 2 * head_size, (pair + 1) * 2 * head_size)
        halves = [
            (
                own_half(k_ref[:, cols], half, head_size),
                own_half(v_ref[:, cols], half, head_size),
            )
            for half in range(2)
        ]
        key_sum = jnp.zeros((patches, 2 * head_size), f32)
        value_sum = jnp.zeros((patches, 2 * head_size), f32)
        for s in range(sources):
            query, grad = ins[2 * s][:, cols], ins[2 * s + 1][:, cols]
            query_t = []
            for half in range(2):
                h = 2 * pair + half
                lam = totals[s][0][h : h + 1]
                delta = totals[s][1][h : h + 1]
                parts = block_products(*halves[half], query, grad, blocks)
                attn_rows, score_rows = [], []
                for j in range(blocks):
                    start = j * CAUSAL_BLOCK
                    attn = jnp.exp2((parts[j][0] - lam[:, start:]) * factor)
                    score_grad = (attn * (parts[j][1] - delta[:, start:])).astype(bf16)
                    attn = attn.astype(bf16)
                    if start:
                        pad = jnp.zeros((CAUSAL_BLOCK, start), bf16)
                        attn = jnp.concatenate([pad, attn], axis=1)
                        score_grad = jnp.concatenate([pad, score_grad], axis=1)
                    attn_rows.append(attn)
                    score_rows.append(score_grad)
                attn = jnp.concatenate(attn_rows, axis=0)
                score_grad = jnp.concatenate(score_rows, axis=0)
                key_sum = key_sum + dot_nn(score_grad, own_half(query, half, head_size))
                value_sum = value_sum + dot_nn(attn, own_half(grad, half, head_size))
                query_t.append(dot_nn(key_t[h * head_size : (h + 1) * head_size], score_grad))
            part = jnp.transpose(jnp.concatenate(query_t, axis=0)) * scale
            if s == 0:
                own_out[:, cols] = part
            else:
                part_outs[s - 1][:, cols] = part.astype(bf16)
        kv_out[0, :, cols] = (key_sum * scale).astype(bf16)
        kv_out[1, :, cols] = value_sum.astype(bf16)


def specs(patches, width):
    token = pl.BlockSpec((patches, width), lambda g: (0, g))
    stat = pl.BlockSpec((1, 2 * GROUP, patches), lambda g: (g, 0, 0))
    flag = pl.BlockSpec(memory_space=pltpu.SMEM)
    return token, stat, flag


def block_stats(linked, keys, values, pairs, head_size, scale):
    patches, features = keys.shape
    token, stat, flag = specs(patches, GROUP * head_size)
    groups = HEADS // GROUP
    n = len(pairs)
    return pl.pallas_call(
        functools.partial(stats_kernel, n, head_size, scale),
        grid=(groups,),
        in_specs=[flag] + [token] * (2 + 2 * n),
        out_specs=[stat] * n,
        out_shape=[jax.ShapeDtypeStruct((groups, 2 * GROUP, patches), f32)] * n,
        compiler_params=pltpu.CompilerParams(vmem_limit_bytes=48 * 2**20),
        cost_estimate=spent(OPT["k1"] * 2.5 * n),
        name="row_stats",
    )(linked, keys, values, *[x for pair in pairs for x in pair])


def block_grads(linked, keys, values, pairs, stats, head_size, scale):
    patches, features = keys.shape
    token, stat, flag = specs(patches, GROUP * head_size)
    groups = HEADS // GROUP
    n = len(pairs)
    window = len(stats[0])
    both = pl.BlockSpec((2, patches, GROUP * head_size), lambda g: (0, 0, g))
    shape = jax.ShapeDtypeStruct
    return pl.pallas_call(
        functools.partial(grads_kernel, n, window, head_size, scale),
        grid=(groups,),
        in_specs=[flag] + [token] * (2 + 2 * n) + [stat] * (n * window),
        out_specs=[token] * n + [both],
        out_shape=[shape((patches, features), f32)]
        + [shape((patches, features), bf16)] * (n - 1)
        + [shape((2, patches, features), bf16)],
        compiler_params=pltpu.CompilerParams(vmem_limit_bytes=48 * 2**20),
        cost_estimate=spent(OPT["k2"] * 4.8 * n),
        name="block_grads",
    )(
        linked,
        keys,
        values,
        *[x for pair in pairs for x in pair],
        *[x for group in stats for x in group],
    )


def place_kernel(at_ref, first_ref, *refs):
    out_ref = refs[-1]
    chunk = first_ref.shape[1] // 3

    def put(at, value):
        col = pl.multiple_of(at * CAUSAL_BLOCK, CAUSAL_BLOCK)
        out_ref[:, pl.ds(col, value.shape[1])] = value

    def put_rolled(at, pieces):
        parts = [
            ref[:, i : i + CAUSAL_BLOCK]
            for ref in pieces
            for i in range(0, ref.shape[1], CAUSAL_BLOCK)
        ]
        for i, part in enumerate(parts):
            put(at + (i + 1) % len(parts), part)

    for i in range(3):
        put(at_ref[3 + i], first_ref[:, i * chunk : (i + 1) * chunk])
    far0_ref, far1_ref, end_ref = refs[:-1]
    put_rolled(at_ref[1], [far0_ref, far1_ref])

    @pl.when(at_ref[0] != 0)
    def _():
        put_rolled(at_ref[2], [end_ref])


def project_kernel(uses, sets, pieces, swaps, flag_ref, *refs):
    tokens, rows = refs[: 2 * sets], refs[2 * sets : 2 * sets + pieces * (1 + swaps)]
    outs = refs[2 * sets + pieces * (1 + swaps) :]
    features = tokens[0].shape[1]
    filled = [0] * sets

    def add(piece, cols):
        step = 256 if piece.shape[0] % 256 == 0 else CAUSAL_BLOCK

        @pl.loop(0, piece.shape[0] // step)
        def _(i):
            part = piece[pl.ds(pl.multiple_of(i * step, step), step), :]
            for t, col in cols:
                at = pl.ds(pl.multiple_of(col + i * step, CAUSAL_BLOCK), step)
                query, pair = tokens[2 * t], tokens[2 * t + 1]
                total = dot_nt(query[...], part[:, :features])
                total = total + dot_nt(pair[0], part[:, features : 2 * features])
                total = total + dot_nt(pair[1], part[:, 2 * features :])
                outs[t][:, at] = total.astype(bf16)

    for p in range(pieces):
        cols = [(t, filled[t]) for t in range(sets) if p in uses[t]]
        if swaps:
            pl.when(flag_ref[0] != 0)(functools.partial(add, rows[p], cols))
            pl.when(flag_ref[0] == 0)(functools.partial(add, rows[pieces + p], cols))
        else:
            add(rows[p], cols)
        for t, _ in cols:
            filled[t] += rows[p].shape[0]


def project(flag, token_sets, rows, other_rows=(), uses=None):
    patches = token_sets[0][0].shape[0]
    uses = uses or [list(range(len(rows)))] * len(token_sets)
    widths = [sum(rows[p].shape[0] for p in use) for use in uses]
    whole = pl.BlockSpec(memory_space=pltpu.VMEM)
    operands = [x for t in token_sets for x in t] + list(rows) + list(other_rows)
    return pl.pallas_call(
        functools.partial(
            project_kernel, uses, len(token_sets), len(rows), 1 if other_rows else 0
        ),
        in_specs=[pl.BlockSpec(memory_space=pltpu.SMEM)] + [whole] * len(operands),
        out_specs=[whole] * len(token_sets),
        out_shape=[jax.ShapeDtypeStruct((patches, width), bf16) for width in widths],
        compiler_params=pltpu.CompilerParams(vmem_limit_bytes=32 * 2**20),
        cost_estimate=spent(OPT["kp"] * (1 + 0.004 * sum(widths))),
        name="project",
    )(flag, *operands)


def times(tokens, rows):
    return dot_nt(tokens, rows).astype(bf16)


def swapped(block):
    return lax.ppermute(block, "dp", [(0, 1), (1, 0)])


def on_line(block, moves):
    return lax.ppermute(
        block, ("var", "dp"), [(a * 2 + c, b * 2 + d) for (a, c), (b, d) in moves]
    )


def attention_grads(queries, keys, values, out_grad, links, reach, sends):
    patches, feature_width = queries.shape
    head_size = feature_width // HEADS
    scale = 1.0 / math.sqrt(head_size)
    n = lax.axis_size("var")
    own = lax.axis_index("var")
    offsets = [0] + [o for d in range(1, reach + 1) for o in (d, -d)]
    pairs = [(queries, out_grad)]
    for o in offsets[1:]:
        pairs.append((passed_along(queries, "var", -o), passed_along(out_grad, "var", -o)))
    sources = (own + jnp.array(offsets, jnp.int32)) % n
    linked = jnp.any(links[sources] == own, axis=1).astype(jnp.int32)
    own_stats = block_stats(linked[:1], keys, values, pairs[:1], head_size, scale)
    sent = sends[0](
        *{
            "first": [pairs[1][0]],
            "own": [own_stats[0]],
            "all": [x for p in pairs[1:] for x in p],
        }[OPT["wa"]]
    )
    other_stats = block_stats(linked[1:], keys, values, pairs[1:], head_size, scale)
    stats = dict(zip(offsets, list(own_stats) + list(other_stats)))
    needed = {}
    for d in offsets:
        for e in offsets:
            entries = needed.setdefault((d + e) % n, [])
            if -e not in entries:
                entries.append(-e)
    arrived, messages = {}, []
    for t, entries in needed.items():
        if t == 0:
            arrived[t] = {o: stats[o] for o in entries}
            continue
        entries.sort()
        message = jnp.stack([stats[o] for o in entries])
        message = passed_along(after(message, *sent) if OPT["st"] else message, "var", -t)
        messages.append(message)
        arrived[t] = {o: message[i] for i, o in enumerate(entries)}
    sent = sends[1](*messages)
    windows = [[arrived[(d + e) % n][-e] for e in offsets] for d in offsets]
    grads = block_grads(linked, keys, values, pairs, windows, head_size, scale)
    returned = [
        passed_along(after(part, *sent) if OPT["dq"] else part, "var", o) for o, part in zip(offsets[1:], grads[1:-1])
    ]
    sent = sends[2](grads[-1])
    query_grad = grads[0]
    for part in returned:
        query_grad = query_grad + part.astype(f32)
    query_grad = query_grad.astype(bf16)
    if OPT["cb"]:
        query_grad = after(query_grad, *sent)
    return query_grad, grads[-1], returned


def shards(queries, keys, values, out_grad, proj_weight, links):
    patches, feature_width = queries.shape[3:]
    n = lax.axis_size("var")
    segments = lax.axis_size("segment")
    reach = min(4, (n - 1) // 2)
    flat = [x.reshape(patches, feature_width) for x in (queries, keys, values, out_grad)]
    weight = proj_weight[0]
    if n != 4:
        query_grad, pair, returned = attention_grads(*flat, links, reach, [lambda *values: ()] * 3)
        grad_qkv = jnp.concatenate([query_grad, pair[0], pair[1]], axis=1)
        whole = lax.all_gather(weight, "var", axis=0, tiled=True)
        passed = passed_along(times(grad_qkv, whole), "segment", -1)
        return passed.reshape(1, 1, 1, patches, whole.shape[0])

    own = lax.axis_index("var")
    core = lax.axis_index("dp")
    chunk = weight.shape[0]
    ends = [0] + OPT["cuts"] + [chunk]
    cuts = list(zip(ends[:-1], ends[1:]))
    step_near = [((v, 0), (v + 1, 0)) for v in range(3)] + [((v + 1, 1), (v, 1)) for v in range(3)]
    step_far = [((1, 0), (2, 0)), ((2, 0), (3, 0)), ((2, 1), (1, 1)), ((1, 1), (0, 1))]
    near, swapped_near = [], {}

    def send_near(i, *values):
        near.append(on_line(after(weight[slice(*cuts[i])], *values), step_near))
        return near[i:]

    far, swapped_far, token = {}, {}, []
    count = len(cuts)

    def ties(names, pair, returned, query_grad):
        have = {
            "pair": lambda: [pair],
            "token": lambda: token,
            "ret0": lambda: returned[:1],
            "ret": lambda: returned,
            "ret1": lambda: returned[1:],
            "sw": lambda: [swapped_near[i] for i in sorted(swapped_near)],
            "nb": lambda: [near[1]],
            "nl": lambda: [near[-1]],
            "q": lambda: [query_grad],
        }
        return [x for name in names.split() for x in have[name]()]

    def start_far(when, *state):
        for i in [int(c) for c in OPT["order"]]:
            if OPT["far"][i][0] == when:
                far[i] = on_line(after(near[i], *ties(OPT["far"][i][1:], *state)), step_far)

    def send_middle(*values):
        sent = send_near(1, *values)
        for i in range(count):
            if OPT["far"][i] == "s":
                far[i] = on_line(after(near[i], *values), step_far)
        return sent

    def send_last(pair):
        token.append(swapped(after(near[0], pair)))
        swapped_near[0] = token[0]
        state = (pair, None, None)
        if count > 2:
            send_near(2, *ties(OPT["nc"], *state))
        for i in range(1, count):
            swapped_near[i] = swapped(after(near[i], pair))
        start_far("e", *state)
        return near[-1:]

    query_grad, pair, returned = attention_grads(
        *flat,
        links,
        reach,
        [lambda *v: send_near(0, *v), send_middle, send_last],
    )
    state = (pair, returned, query_grad)
    start_far("l", *state)
    inward = [(0, 1), (3, 2)]
    outer_pair = lax.ppermute(after(pair, *ties(OPT["op"], *state)), "var", inward)
    outer_query = lax.ppermute(query_grad, "var", inward)
    far_here = (core == jnp.where(own < 2, 1, 0)).astype(jnp.int32).reshape(1)

    def handed_on(block, moves):
        route = [(a * segments + s, b * segments + (s - 1) % segments) for a, b in moves for s in range(segments)]
        return lax.ppermute(block, ("var", "segment"), route)

    in_place = [(v, v) for v in range(4)]
    from_inner = [(1, 0), (2, 3)]
    own_set, outer_set = (query_grad, pair), (outer_query, outer_pair)
    (result,) = project(far_here, [own_set], [weight] + near + [swapped_near[i] for i in range(count)])
    first = handed_on(result, in_place)
    if OPT.get("one"):
        joined = jnp.concatenate([near[1][256:], near[0]], axis=0)
        rows = [near[1][:256], joined]
        far = [on_line(after(r, *ties(OPT["ft"][i], *state)), step_far) for i, r in enumerate(rows)]
    have = {"r": result, "f": first, "p": outer_pair, "q": outer_query}
    ties_of = [have[c] for c in OPT["sf"]]
    other0 = swapped(after(far[0], *ties_of))
    (far0,) = project(far_here, [own_set], far[:1], [other0])
    handed0 = handed_on(far0, in_place)
    have.update(x=far0, h=handed0)
    other1 = swapped(after(far[1], *[have[c] for c in OPT["s1"]]))
    far1, end = project(
        far_here, [own_set, outer_set], far, [other0, other1], [[1], [0, 1]]
    )
    parts = [handed0, handed_on(far1, in_place), handed_on(end, from_inner)]

    is_end = (own == 0) | (own == 3)
    blocks = chunk // CAUSAL_BLOCK
    far_at = (own + 2) % 4 * blocks
    end_at = jnp.where(is_end, 3 - own, (own + 2) % 4) * blocks
    places = jnp.stack(
        [
            is_end.astype(jnp.int32),
            far_at,
            end_at,
            own * blocks,
            (own + 3 + 2 * core) % 4 * blocks,
            (own + 1 + 2 * core) % 4 * blocks,
        ]
    ).astype(jnp.int32)
    whole = pl.BlockSpec(memory_space=pltpu.VMEM)
    passed = pl.pallas_call(
        place_kernel,
        in_specs=[pl.BlockSpec(memory_space=pltpu.SMEM)] + [whole] * (1 + len(parts)),
        out_specs=whole,
        out_shape=jax.ShapeDtypeStruct((patches, 4 * chunk), bf16),
        name="placed",
    )(places, first, *parts)
    return passed.reshape(1, 1, 1, patches, 4 * chunk)


def solution(mesh):
    return jax.shard_map(
        shards,
        mesh=mesh,
        in_specs=(
            P("dp", "segment", "var", None, None),
            P("dp", "segment", "var", None, None),
            P("dp", "segment", "var", None, None),
            P("dp", "segment", "var", None, None),
            P("segment", "var", None),
            P(),
        ),
        out_specs=P("dp", "segment", "var", None, None),
        check_vma=False,
    )
```

```python
import functools
import math

import jax
import jax.numpy as jnp
from jax import lax
from jax.experimental import pallas as pl
from jax.experimental.pallas import tpu as pltpu
from jax.sharding import PartitionSpec as P

HEADS = 16
CAUSAL_BLOCK = 128
GROUP = 4

neg_big = -1e30
f32 = jnp.float32
bf16 = jnp.bfloat16


def passed_along(block, axis, distance):
    devices = range(lax.axis_size(axis))
    route = [((i - distance) % len(devices), i) for i in devices]
    return lax.ppermute(block, axis, route)


def spent(us):
    return pl.CostEstimate(flops=int(us * 1.15e9), bytes_accessed=1024, transcendentals=0)


def after(block, *earlier):
    return lax.optimization_barrier((block,) + earlier)[0]


def dot_nt(a, b):
    return lax.dot_general(a, b, (((1,), (1,)), ((), ())), preferred_element_type=f32)


def dot_nn(a, b):
    return lax.dot_general(a, b, (((1,), (0,)), ((), ())), preferred_element_type=f32)


def own_half(block, half, head_size):
    lane = lax.broadcasted_iota(jnp.int32, block.shape, 1)
    keep = (lane < head_size) if half == 0 else (lane >= head_size)
    return jnp.where(keep, block, jnp.zeros_like(block))


def block_products(key_half, value_half, query, grad, blocks):
    out = []
    for j in range(blocks):
        rows = slice(j * CAUSAL_BLOCK, (j + 1) * CAUSAL_BLOCK)
        start = j * CAUSAL_BLOCK
        out.append(
            (dot_nt(key_half[rows], query[start:]), dot_nt(value_half[rows], grad[start:]))
        )
    return out


def stats_kernel(sources, head_size, scale, linked_ref, k_ref, v_ref, *refs):
    ins, outs = refs[: 2 * sources], refs[2 * sources :]
    patches = k_ref.shape[0]
    blocks = patches // CAUSAL_BLOCK
    factor = scale * math.log2(math.e)
    for s in range(sources):
        linked = linked_ref[s] != 0
        lams, deltas = [], []
        for h in range(GROUP):
            cols = slice((h // 2) * 2 * head_size, (h // 2 + 1) * 2 * head_size)
            key_half = own_half(k_ref[:, cols], h % 2, head_size)
            value_half = own_half(v_ref[:, cols], h % 2, head_size)
            parts = block_products(
                key_half, value_half, ins[2 * s][:, cols], ins[2 * s + 1][:, cols], blocks
            )
            lam_row, delta_row = [], []
            for i in range(blocks):
                pieces = []
                for j in range(i + 1):
                    at = slice((i - j) * CAUSAL_BLOCK, (i - j + 1) * CAUSAL_BLOCK)
                    pieces.append((parts[j][0][:, at], parts[j][1][:, at]))
                top = functools.reduce(
                    jnp.maximum, [jnp.max(p[0], axis=0, keepdims=True) for p in pieces]
                )
                total = 0.0
                weighted = 0.0
                for score, grad_attn in pieces:
                    e = jnp.exp2((score - top) * factor)
                    total = total + jnp.sum(e, axis=0, keepdims=True)
                    weighted = weighted + jnp.sum(e * grad_attn, axis=0, keepdims=True)
                lam_row.append(top + jnp.log(total) * (1.0 / scale))
                delta_row.append(weighted / total)
            lams.append(jnp.concatenate(lam_row, axis=1))
            deltas.append(jnp.concatenate(delta_row, axis=1))
        lam = jnp.where(linked, jnp.concatenate(lams, axis=0), neg_big)
        delta = jnp.where(linked, jnp.concatenate(deltas, axis=0), 0.0)
        outs[s][0] = jnp.concatenate([lam, delta], axis=0)


def grads_kernel(sources, window, head_size, scale, linked_ref, k_ref, v_ref, *refs):
    ins = refs[: 2 * sources]
    stats = refs[2 * sources : 2 * sources + sources * window]
    outs = refs[2 * sources + sources * window :]
    own_out, part_outs, kv_out = outs[0], outs[1:sources], outs[sources]
    patches = k_ref.shape[0]
    blocks = patches // CAUSAL_BLOCK
    factor = scale * math.log2(math.e)
    key_t = jnp.transpose(k_ref[...].astype(f32)).astype(bf16)
    totals = []
    for s in range(sources):
        lams = [r[0, :GROUP] for r in stats[s * window : (s + 1) * window]]
        deltas = [r[0, GROUP:] for r in stats[s * window : (s + 1) * window]]
        top = functools.reduce(jnp.maximum, lams)
        weights = [jnp.exp2((lam - top) * factor) for lam in lams]
        total = functools.reduce(jnp.add, weights)
        delta = functools.reduce(jnp.add, [w * d for w, d in zip(weights, deltas)]) / total
        lam = top + jnp.log(total) * (1.0 / scale)
        lam = jnp.where(linked_ref[s] != 0, lam, -neg_big)
        totals.append((lam, delta))
    for pair in range(GROUP // 2):
        cols = slice(pair * 2 * head_size, (pair + 1) * 2 * head_size)
        halves = [
            (
                own_half(k_ref[:, cols], half, head_size),
                own_half(v_ref[:, cols], half, head_size),
            )
            for half in range(2)
        ]
        key_sum = jnp.zeros((patches, 2 * head_size), f32)
        value_sum = jnp.zeros((patches, 2 * head_size), f32)
        for s in range(sources):
            query, grad = ins[2 * s][:, cols], ins[2 * s + 1][:, cols]
            query_t = []
            for half in range(2):
                h = 2 * pair + half
                lam = totals[s][0][h : h + 1]
                delta = totals[s][1][h : h + 1]
                parts = block_products(*halves[half], query, grad, blocks)
                attn_rows, score_rows = [], []
                for j in range(blocks):
                    start = j * CAUSAL_BLOCK
                    attn = jnp.exp2((parts[j][0] - lam[:, start:]) * factor)
                    score_grad = (attn * (parts[j][1] - delta[:, start:])).astype(bf16)
                    attn = attn.astype(bf16)
                    if start:
                        pad = jnp.zeros((CAUSAL_BLOCK, start), bf16)
                        attn = jnp.concatenate([pad, attn], axis=1)
                        score_grad = jnp.concatenate([pad, score_grad], axis=1)
                    attn_rows.append(attn)
                    score_rows.append(score_grad)
                attn = jnp.concatenate(attn_rows, axis=0)
                score_grad = jnp.concatenate(score_rows, axis=0)
                key_sum = key_sum + dot_nn(score_grad, own_half(query, half, head_size))
                value_sum = value_sum + dot_nn(attn, own_half(grad, half, head_size))
                query_t.append(dot_nn(key_t[h * head_size : (h + 1) * head_size], score_grad))
            part = jnp.transpose(jnp.concatenate(query_t, axis=0)) * scale
            if s == 0:
                own_out[:, cols] = part
            else:
                part_outs[s - 1][:, cols] = part.astype(bf16)
        kv_out[0, :, cols] = (key_sum * scale).astype(bf16)
        kv_out[1, :, cols] = value_sum.astype(bf16)


def specs(patches, width):
    token = pl.BlockSpec((patches, width), lambda g: (0, g))
    stat = pl.BlockSpec((1, 2 * GROUP, patches), lambda g: (g, 0, 0))
    flag = pl.BlockSpec(memory_space=pltpu.SMEM)
    return token, stat, flag


def block_stats(linked, keys, values, pairs, head_size, scale):
    patches, features = keys.shape
    token, stat, flag = specs(patches, GROUP * head_size)
    groups = HEADS // GROUP
    n = len(pairs)
    return pl.pallas_call(
        functools.partial(stats_kernel, n, head_size, scale),
        grid=(groups,),
        in_specs=[flag] + [token] * (2 + 2 * n),
        out_specs=[stat] * n,
        out_shape=[jax.ShapeDtypeStruct((groups, 2 * GROUP, patches), f32)] * n,
        compiler_params=pltpu.CompilerParams(vmem_limit_bytes=48 * 2**20),
        cost_estimate=spent(0.025 * n),
        name="row_stats",
    )(linked, keys, values, *[x for pair in pairs for x in pair])


def block_grads(linked, keys, values, pairs, stats, head_size, scale):
    patches, features = keys.shape
    token, stat, flag = specs(patches, GROUP * head_size)
    groups = HEADS // GROUP
    n = len(pairs)
    window = len(stats[0])
    both = pl.BlockSpec((2, patches, GROUP * head_size), lambda g: (0, 0, g))
    shape = jax.ShapeDtypeStruct
    return pl.pallas_call(
        functools.partial(grads_kernel, n, window, head_size, scale),
        grid=(groups,),
        in_specs=[flag] + [token] * (2 + 2 * n) + [stat] * (n * window),
        out_specs=[token] * n + [both],
        out_shape=[shape((patches, features), f32)]
        + [shape((patches, features), bf16)] * (n - 1)
        + [shape((2, patches, features), bf16)],
        compiler_params=pltpu.CompilerParams(vmem_limit_bytes=48 * 2**20),
        cost_estimate=spent(48 * n),
        name="block_grads",
    )(
        linked,
        keys,
        values,
        *[x for pair in pairs for x in pair],
        *[x for group in stats for x in group],
    )


def place_kernel(roll, first_ref, *refs):
    far_refs, end_ref, out_ref = refs[:-2], refs[-2], refs[-1]
    chunk = end_ref.shape[1]
    own, core = lax.axis_index("var"), lax.axis_index("dp")
    is_end = (own == 0) | (own == 3)

    def put(ref, start, width, at, shift):
        col = pl.multiple_of(at * chunk + shift, CAUSAL_BLOCK)
        out_ref[:, pl.ds(col, width)] = ref[:, start : start + width]

    def put_rolled(pieces, at):
        shift = roll
        for ref in pieces:
            width = ref.shape[1]
            edge = min(width, chunk - shift)
            put(ref, 0, edge, at, shift)
            if edge < width:
                put(ref, edge, width - edge, at, 0)
            shift += width

    for i, at in enumerate(
        [own, lax.rem(own + 3 + 2 * core, 4), lax.rem(own + 1 + 2 * core, 4)]
    ):
        put(first_ref, i * chunk, chunk, at, 0)
    put_rolled(far_refs, lax.rem(own + 2, 4))
    pl.when(is_end)(lambda: put_rolled([end_ref], 3 - own))


def project_kernel(uses, sets, pieces, swaps, flag_ref, *refs):
    tokens, rows = refs[: 2 * sets], refs[2 * sets : 2 * sets + pieces * (1 + swaps)]
    outs = refs[2 * sets + pieces * (1 + swaps) :]
    features = tokens[0].shape[1]
    filled = [0] * sets

    def add(piece, cols):
        step = 256 if piece.shape[0] % 256 == 0 else CAUSAL_BLOCK

        @pl.loop(0, piece.shape[0] // step)
        def _(i):
            part = piece[pl.ds(pl.multiple_of(i * step, step), step), :]
            for t, col in cols:
                at = pl.ds(pl.multiple_of(col + i * step, CAUSAL_BLOCK), step)
                query, pair = tokens[2 * t], tokens[2 * t + 1]
                total = dot_nt(query[...], part[:, :features])
                total = total + dot_nt(pair[0], part[:, features : 2 * features])
                total = total + dot_nt(pair[1], part[:, 2 * features :])
                outs[t][:, at] = total.astype(bf16)

    for p in range(pieces):
        cols = [(t, filled[t]) for t in range(sets) if p in uses[t]]
        if swaps:
            pl.when(flag_ref[0] != 0)(functools.partial(add, rows[p], cols))
            pl.when(flag_ref[0] == 0)(functools.partial(add, rows[pieces + p], cols))
        else:
            add(rows[p], cols)
        for t, _ in cols:
            filled[t] += rows[p].shape[0]


def project(flag, token_sets, rows, other_rows=(), uses=None):
    patches = token_sets[0][0].shape[0]
    uses = uses or [list(range(len(rows)))] * len(token_sets)
    widths = [sum(rows[p].shape[0] for p in use) for use in uses]
    whole = pl.BlockSpec(memory_space=pltpu.VMEM)
    operands = [x for t in token_sets for x in t] + list(rows) + list(other_rows)
    return pl.pallas_call(
        functools.partial(
            project_kernel, uses, len(token_sets), len(rows), 1 if other_rows else 0
        ),
        in_specs=[pl.BlockSpec(memory_space=pltpu.SMEM)] + [whole] * len(operands),
        out_specs=[whole] * len(token_sets),
        out_shape=[jax.ShapeDtypeStruct((patches, width), bf16) for width in widths],
        compiler_params=pltpu.CompilerParams(vmem_limit_bytes=32 * 2**20),
        cost_estimate=spent(1 + 0.004 * sum(widths)),
        name="project",
    )(flag, *operands)


def times(tokens, rows):
    return dot_nt(tokens, rows).astype(bf16)


def swapped(block):
    return lax.ppermute(block, "dp", [(0, 1), (1, 0)])


def on_line(block, moves):
    return lax.ppermute(
        block, ("var", "dp"), [(a * 2 + c, b * 2 + d) for (a, c), (b, d) in moves]
    )


def attention_grads(queries, keys, values, out_grad, links, reach, sends):
    patches, feature_width = queries.shape
    head_size = feature_width // HEADS
    scale = 1.0 / math.sqrt(head_size)
    n = lax.axis_size("var")
    own = lax.axis_index("var")
    offsets = [0] + [o for d in range(1, reach + 1) for o in (d, -d)]
    pairs = [(queries, out_grad)]
    for o in offsets[1:]:
        pairs.append((passed_along(queries, "var", -o), passed_along(out_grad, "var", -o)))
    sources = (own + jnp.array(offsets, jnp.int32)) % n
    linked = jnp.any(links[sources] == own, axis=1).astype(jnp.int32)
    own_stats = block_stats(linked[:1], keys, values, pairs[:1], head_size, scale)
    first_sent = sends[0](own_stats[0])
    other_stats = block_stats(linked[1:], keys, values, pairs[1:], head_size, scale)
    stats = dict(zip(offsets, list(own_stats) + list(other_stats)))
    needed = {}
    for d in offsets:
        for e in offsets:
            entries = needed.setdefault((d + e) % n, [])
            if -e not in entries:
                entries.append(-e)
    arrived, messages = {}, []
    for t, entries in needed.items():
        if t == 0:
            arrived[t] = {o: stats[o] for o in entries}
            continue
        entries.sort()
        message = jnp.stack([stats[o] for o in entries])
        message = passed_along(message, "var", -t)
        messages.append(message)
        arrived[t] = {o: message[i] for i, o in enumerate(entries)}
    sent = sends[1](messages[0])
    windows = [[arrived[(d + e) % n][-e] for e in offsets] for d in offsets]
    linked = after(linked, *first_sent)
    grads = block_grads(linked, keys, values, pairs, windows, head_size, scale)
    returned = [
        passed_along(after(part, *sent), "var", o)
        for o, part in zip(offsets[1:], grads[1:-1])
    ]
    sends[2](grads[-1])
    query_grad = grads[0]
    for part in returned:
        query_grad = query_grad + part.astype(f32)
    return query_grad.astype(bf16), grads[-1], returned


def shards(queries, keys, values, out_grad, proj_weight, links):
    patches, feature_width = queries.shape[3:]
    n = lax.axis_size("var")
    segments = lax.axis_size("segment")
    reach = min(4, (n - 1) // 2)
    flat = [x.reshape(patches, feature_width) for x in (queries, keys, values, out_grad)]
    weight = proj_weight[0]
    if n != 4:
        query_grad, pair, _ = attention_grads(*flat, links, reach, [lambda value: ()] * 3)
        grad_qkv = jnp.concatenate([query_grad, pair[0], pair[1]], axis=1)
        whole = lax.all_gather(weight, "var", axis=0, tiled=True)
        passed = passed_along(times(grad_qkv, whole), "segment", -1)
        return passed.reshape(1, 1, 1, patches, whole.shape[0])

    own = lax.axis_index("var")
    core = lax.axis_index("dp")
    chunk = weight.shape[0]
    cuts = [(0, CAUSAL_BLOCK), (CAUSAL_BLOCK, chunk)]
    step_near = [((v, 0), (v + 1, 0)) for v in range(3)] + [((v + 1, 1), (v, 1)) for v in range(3)]
    step_far = [((1, 0), (2, 0)), ((2, 0), (3, 0)), ((2, 1), (1, 1)), ((1, 1), (0, 1))]
    pieces = [weight[lo:hi] for lo, hi in cuts]
    near, swapped_near = [], []

    def send_first(value):
        pieces[:] = lax.optimization_barrier((*pieces, value))[:2]
        near.append(on_line(pieces[0], step_near))
        return near[:1]

    def send_second(value):
        near.append(on_line(after(pieces[1], value), step_near))
        return near[1:]

    def swap_near(value):
        swapped_near.extend(swapped(after(piece, value)) for piece in near)

    query_grad, pair, returned = attention_grads(
        *flat, links, reach, [send_first, send_second, swap_near]
    )
    inward = [(0, 1), (3, 2)]
    outer_pair = lax.ppermute(after(pair, returned[1]), "var", inward)
    outer_query = lax.ppermute(query_grad, "var", inward)
    far_here = (core == jnp.where(own < 2, 1, 0)).astype(jnp.int32).reshape(1)

    def handed_on(block, moves):
        route = [
            (a * segments + s, b * segments + (s - 1) % segments)
            for a, b in moves
            for s in range(segments)
        ]
        return lax.ppermute(block, ("var", "segment"), route)

    in_place = [(v, v) for v in range(4)]
    from_inner = [(1, 0), (2, 3)]
    own_set, outer_set = (query_grad, pair), (outer_query, outer_pair)
    (result,) = project(far_here, [own_set], [weight] + near + swapped_near)
    first = handed_on(result, in_place)
    joined = jnp.concatenate([near[1][chunk // 2 :], near[0]], axis=0)
    far = [
        on_line(after(rows, returned[1]), step_far) for rows in (near[1][: chunk // 2], joined)
    ]
    swapped_far = [
        swapped(after(far[0], result)),
        swapped(after(far[1], result, first, outer_pair, outer_query)),
    ]
    far_result, end = project(far_here, [own_set, outer_set], far, swapped_far)
    parts = [handed_on(far_result, in_place), handed_on(end, from_inner)]
    passed = pl.pallas_call(
        functools.partial(place_kernel, CAUSAL_BLOCK),
        in_specs=[pl.BlockSpec(memory_space=pltpu.VMEM)] * (1 + len(parts)),
        out_specs=pl.BlockSpec(memory_space=pltpu.VMEM),
        out_shape=jax.ShapeDtypeStruct((patches, 4 * chunk), bf16),
        name="placed",
    )(first, *parts)
    return passed.reshape(1, 1, 1, patches, 4 * chunk)


def solution(mesh):
    return jax.shard_map(
        shards,
        mesh=mesh,
        in_specs=(
            P("dp", "segment", "var", None, None),
            P("dp", "segment", "var", None, None),
            P("dp", "segment", "var", None, None),
            P("dp", "segment", "var", None, None),
            P("segment", "var", None),
            P(),
        ),
        out_specs=P("dp", "segment", "var", None, None),
        check_vma=False,
    )
```

```python
import functools
import math

import jax
import jax.numpy as jnp
from jax import lax
from jax.experimental import pallas as pl
from jax.experimental.pallas import tpu as pltpu
from jax.sharding import PartitionSpec as P

HEADS = 16
CAUSAL_BLOCK = 128
GROUP = 4

neg_big = -1e30
f32 = jnp.float32
bf16 = jnp.bfloat16


def passed_along(block, axis, distance):
    devices = range(lax.axis_size(axis))
    route = [((i - distance) % len(devices), i) for i in devices]
    return lax.ppermute(block, axis, route)


def spent(us):
    return pl.CostEstimate(flops=int(us * 1.15e9), bytes_accessed=1024, transcendentals=0)


def after(block, *earlier):
    return lax.optimization_barrier((block,) + earlier)[0]


def dot_nt(a, b):
    return lax.dot_general(a, b, (((1,), (1,)), ((), ())), preferred_element_type=f32)


def dot_nn(a, b):
    return lax.dot_general(a, b, (((1,), (0,)), ((), ())), preferred_element_type=f32)


def own_half(block, half, head_size):
    lane = lax.broadcasted_iota(jnp.int32, block.shape, 1)
    keep = (lane < head_size) if half == 0 else (lane >= head_size)
    return jnp.where(keep, block, jnp.zeros_like(block))


def block_products(key_half, value_half, query, grad, blocks):
    out = []
    for j in range(blocks):
        rows = slice(j * CAUSAL_BLOCK, (j + 1) * CAUSAL_BLOCK)
        start = j * CAUSAL_BLOCK
        out.append(
            (dot_nt(key_half[rows], query[start:]), dot_nt(value_half[rows], grad[start:]))
        )
    return out


def stats_kernel(sources, head_size, scale, linked_ref, k_ref, v_ref, *refs):
    ins, outs = refs[: 2 * sources], refs[2 * sources :]
    patches = k_ref.shape[0]
    blocks = patches // CAUSAL_BLOCK
    factor = scale * math.log2(math.e)
    for s in range(sources):
        linked = linked_ref[s] != 0
        lams, deltas = [], []
        for h in range(GROUP):
            cols = slice((h // 2) * 2 * head_size, (h // 2 + 1) * 2 * head_size)
            key_half = own_half(k_ref[:, cols], h % 2, head_size)
            value_half = own_half(v_ref[:, cols], h % 2, head_size)
            parts = block_products(
                key_half, value_half, ins[2 * s][:, cols], ins[2 * s + 1][:, cols], blocks
            )
            lam_row, delta_row = [], []
            for i in range(blocks):
                pieces = []
                for j in range(i + 1):
                    at = slice((i - j) * CAUSAL_BLOCK, (i - j + 1) * CAUSAL_BLOCK)
                    pieces.append((parts[j][0][:, at], parts[j][1][:, at]))
                top = functools.reduce(
                    jnp.maximum, [jnp.max(p[0], axis=0, keepdims=True) for p in pieces]
                )
                total = 0.0
                weighted = 0.0
                for score, grad_attn in pieces:
                    e = jnp.exp2((score - top) * factor)
                    total = total + jnp.sum(e, axis=0, keepdims=True)
                    weighted = weighted + jnp.sum(e * grad_attn, axis=0, keepdims=True)
                lam_row.append(top + jnp.log(total) * (1.0 / scale))
                delta_row.append(weighted / total)
            lams.append(jnp.concatenate(lam_row, axis=1))
            deltas.append(jnp.concatenate(delta_row, axis=1))
        lam = jnp.where(linked, jnp.concatenate(lams, axis=0), neg_big)
        delta = jnp.where(linked, jnp.concatenate(deltas, axis=0), 0.0)
        outs[s][0] = jnp.concatenate([lam, delta], axis=0)


def grads_kernel(sources, window, head_size, scale, linked_ref, k_ref, v_ref, *refs):
    ins = refs[: 2 * sources]
    stats = refs[2 * sources : 2 * sources + sources * window]
    outs = refs[2 * sources + sources * window :]
    own_out, part_outs, kv_out = outs[0], outs[1:sources], outs[sources]
    patches = k_ref.shape[0]
    blocks = patches // CAUSAL_BLOCK
    factor = scale * math.log2(math.e)
    key_t = jnp.transpose(k_ref[...].astype(f32)).astype(bf16)
    totals = []
    for s in range(sources):
        lams = [r[0, :GROUP] for r in stats[s * window : (s + 1) * window]]
        deltas = [r[0, GROUP:] for r in stats[s * window : (s + 1) * window]]
        top = functools.reduce(jnp.maximum, lams)
        weights = [jnp.exp2((lam - top) * factor) for lam in lams]
        total = functools.reduce(jnp.add, weights)
        delta = functools.reduce(jnp.add, [w * d for w, d in zip(weights, deltas)]) / total
        lam = top + jnp.log(total) * (1.0 / scale)
        lam = jnp.where(linked_ref[s] != 0, lam, -neg_big)
        totals.append((lam, delta))
    for pair in range(GROUP // 2):
        cols = slice(pair * 2 * head_size, (pair + 1) * 2 * head_size)
        halves = [
            (
                own_half(k_ref[:, cols], half, head_size),
                own_half(v_ref[:, cols], half, head_size),
            )
            for half in range(2)
        ]
        key_sum = jnp.zeros((patches, 2 * head_size), f32)
        value_sum = jnp.zeros((patches, 2 * head_size), f32)
        for s in range(sources):
            query, grad = ins[2 * s][:, cols], ins[2 * s + 1][:, cols]
            query_t = []
            for half in range(2):
                h = 2 * pair + half
                lam = totals[s][0][h : h + 1]
                delta = totals[s][1][h : h + 1]
                parts = block_products(*halves[half], query, grad, blocks)
                attn_rows, score_rows = [], []
                for j in range(blocks):
                    start = j * CAUSAL_BLOCK
                    attn = jnp.exp2((parts[j][0] - lam[:, start:]) * factor)
                    score_grad = (attn * (parts[j][1] - delta[:, start:])).astype(bf16)
                    attn = attn.astype(bf16)
                    if start:
                        pad = jnp.zeros((CAUSAL_BLOCK, start), bf16)
                        attn = jnp.concatenate([pad, attn], axis=1)
                        score_grad = jnp.concatenate([pad, score_grad], axis=1)
                    attn_rows.append(attn)
                    score_rows.append(score_grad)
                attn = jnp.concatenate(attn_rows, axis=0)
                score_grad = jnp.concatenate(score_rows, axis=0)
                key_sum = key_sum + dot_nn(score_grad, own_half(query, half, head_size))
                value_sum = value_sum + dot_nn(attn, own_half(grad, half, head_size))
                query_t.append(dot_nn(key_t[h * head_size : (h + 1) * head_size], score_grad))
            part = jnp.transpose(jnp.concatenate(query_t, axis=0)) * scale
            if s == 0:
                own_out[:, cols] = part
            else:
                part_outs[s - 1][:, cols] = part.astype(bf16)
        kv_out[0, :, cols] = (key_sum * scale).astype(bf16)
        kv_out[1, :, cols] = value_sum.astype(bf16)


def specs(patches, width):
    token = pl.BlockSpec((patches, width), lambda g: (0, g))
    stat = pl.BlockSpec((1, 2 * GROUP, patches), lambda g: (g, 0, 0))
    flag = pl.BlockSpec(memory_space=pltpu.SMEM)
    return token, stat, flag


def block_stats(linked, keys, values, pairs, head_size, scale):
    patches, features = keys.shape
    token, stat, flag = specs(patches, GROUP * head_size)
    groups = HEADS // GROUP
    n = len(pairs)
    return pl.pallas_call(
        functools.partial(stats_kernel, n, head_size, scale),
        grid=(groups,),
        in_specs=[flag] + [token] * (2 + 2 * n),
        out_specs=[stat] * n,
        out_shape=[jax.ShapeDtypeStruct((groups, 2 * GROUP, patches), f32)] * n,
        compiler_params=pltpu.CompilerParams(vmem_limit_bytes=48 * 2**20),
        cost_estimate=spent(0.025 * n),
        name="row_stats",
    )(linked, keys, values, *[x for pair in pairs for x in pair])


def block_grads(linked, keys, values, pairs, stats, head_size, scale):
    patches, features = keys.shape
    token, stat, flag = specs(patches, GROUP * head_size)
    groups = HEADS // GROUP
    n = len(pairs)
    window = len(stats[0])
    both = pl.BlockSpec((2, patches, GROUP * head_size), lambda g: (0, 0, g))
    shape = jax.ShapeDtypeStruct
    return pl.pallas_call(
        functools.partial(grads_kernel, n, window, head_size, scale),
        grid=(groups,),
        in_specs=[flag] + [token] * (2 + 2 * n) + [stat] * (n * window),
        out_specs=[token] * n + [both],
        out_shape=[shape((patches, features), f32)]
        + [shape((patches, features), bf16)] * (n - 1)
        + [shape((2, patches, features), bf16)],
        compiler_params=pltpu.CompilerParams(vmem_limit_bytes=48 * 2**20),
        cost_estimate=spent(48 * n),
        name="block_grads",
    )(
        linked,
        keys,
        values,
        *[x for pair in pairs for x in pair],
        *[x for group in stats for x in group],
    )


def place_kernel(roll, first_ref, *refs):
    far_refs, end_refs, out_ref = refs[:2], refs[2:4], refs[4]
    chunk = far_refs[0].shape[1] + far_refs[1].shape[1]
    own, core = lax.axis_index("var"), lax.axis_index("dp")
    is_end = (own == 0) | (own == 3)

    def put(ref, start, width, at, shift):
        col = pl.multiple_of(at * chunk + shift, CAUSAL_BLOCK)
        out_ref[:, pl.ds(col, width)] = ref[:, start : start + width]

    def put_rolled(pieces, at):
        shift = roll
        for ref in pieces:
            width = ref.shape[1]
            edge = min(width, chunk - shift)
            put(ref, 0, edge, at, shift)
            if edge < width:
                put(ref, edge, width - edge, at, 0)
            shift += width

    for i, at in enumerate(
        [own, lax.rem(own + 3 + 2 * core, 4), lax.rem(own + 1 + 2 * core, 4)]
    ):
        put(first_ref, i * chunk, chunk, at, 0)
    put_rolled(far_refs, lax.rem(own + 2, 4))
    pl.when(is_end)(lambda: put_rolled(end_refs, 3 - own))


def project_kernel(uses, sets, pieces, swaps, flag_ref, *refs):
    tokens, rows = refs[: 2 * sets], refs[2 * sets : 2 * sets + pieces * (1 + swaps)]
    outs = refs[2 * sets + pieces * (1 + swaps) :]
    features = tokens[0].shape[1]
    filled = [0] * sets

    def add(piece, cols):
        step = 256 if piece.shape[0] % 256 == 0 else CAUSAL_BLOCK

        @pl.loop(0, piece.shape[0] // step)
        def _(i):
            part = piece[pl.ds(pl.multiple_of(i * step, step), step), :]
            for t, col in cols:
                at = pl.ds(pl.multiple_of(col + i * step, CAUSAL_BLOCK), step)
                query, pair = tokens[2 * t], tokens[2 * t + 1]
                total = dot_nt(query[...], part[:, :features])
                total = total + dot_nt(pair[0], part[:, features : 2 * features])
                total = total + dot_nt(pair[1], part[:, 2 * features :])
                outs[t][:, at] = total.astype(bf16)

    for p in range(pieces):
        cols = [(t, filled[t]) for t in range(sets) if p in uses[t]]
        if swaps:
            pl.when(flag_ref[0] != 0)(functools.partial(add, rows[p], cols))
            pl.when(flag_ref[0] == 0)(functools.partial(add, rows[pieces + p], cols))
        else:
            add(rows[p], cols)
        for t, _ in cols:
            filled[t] += rows[p].shape[0]


def project(flag, token_sets, rows, other_rows=(), uses=None):
    patches = token_sets[0][0].shape[0]
    uses = uses or [list(range(len(rows)))] * len(token_sets)
    widths = [sum(rows[p].shape[0] for p in use) for use in uses]
    whole = pl.BlockSpec(memory_space=pltpu.VMEM)
    operands = [x for t in token_sets for x in t] + list(rows) + list(other_rows)
    return pl.pallas_call(
        functools.partial(
            project_kernel, uses, len(token_sets), len(rows), 1 if other_rows else 0
        ),
        in_specs=[pl.BlockSpec(memory_space=pltpu.SMEM)] + [whole] * len(operands),
        out_specs=[whole] * len(token_sets),
        out_shape=[jax.ShapeDtypeStruct((patches, width), bf16) for width in widths],
        compiler_params=pltpu.CompilerParams(vmem_limit_bytes=32 * 2**20),
        cost_estimate=spent(1 + 0.004 * sum(widths)),
        name="project",
    )(flag, *operands)


def times(tokens, rows):
    return dot_nt(tokens, rows).astype(bf16)


def swapped(block):
    return lax.ppermute(block, "dp", [(0, 1), (1, 0)])


def on_line(block, moves):
    return lax.ppermute(
        block, ("var", "dp"), [(a * 2 + c, b * 2 + d) for (a, c), (b, d) in moves]
    )


def attention_grads(queries, keys, values, out_grad, links, reach, sends):
    patches, feature_width = queries.shape
    head_size = feature_width // HEADS
    scale = 1.0 / math.sqrt(head_size)
    n = lax.axis_size("var")
    own = lax.axis_index("var")
    offsets = [0] + [o for d in range(1, reach + 1) for o in (d, -d)]
    pairs = [(queries, out_grad)]
    for o in offsets[1:]:
        pairs.append((passed_along(queries, "var", -o), passed_along(out_grad, "var", -o)))
    sources = (own + jnp.array(offsets, jnp.int32)) % n
    linked = jnp.any(links[sources] == own, axis=1).astype(jnp.int32)
    own_stats = block_stats(linked[:1], keys, values, pairs[:1], head_size, scale)
    first_sent = sends[0](own_stats[0])
    other_stats = block_stats(linked[1:], keys, values, pairs[1:], head_size, scale)
    stats = dict(zip(offsets, list(own_stats) + list(other_stats)))
    needed = {}
    for d in offsets:
        for e in offsets:
            entries = needed.setdefault((d + e) % n, [])
            if -e not in entries:
                entries.append(-e)
    arrived, messages = {}, []
    for t, entries in needed.items():
        if t == 0:
            arrived[t] = {o: stats[o] for o in entries}
            continue
        entries.sort()
        message = jnp.stack([stats[o] for o in entries])
        message = passed_along(message, "var", -t)
        messages.append(message)
        arrived[t] = {o: message[i] for i, o in enumerate(entries)}
    sends[1](messages[0])
    windows = [[arrived[(d + e) % n][-e] for e in offsets] for d in offsets]
    linked = after(linked, *first_sent)
    grads = block_grads(linked, keys, values, pairs, windows, head_size, scale)
    returned = [
        passed_along(part, "var", o) for o, part in zip(offsets[1:], grads[1:-1])
    ]
    sends[2](returned[-1])
    query_grad = grads[0]
    for part in returned:
        query_grad = query_grad + part.astype(f32)
    return query_grad.astype(bf16), grads[-1], returned


def shards(queries, keys, values, out_grad, proj_weight, links):
    patches, feature_width = queries.shape[3:]
    n = lax.axis_size("var")
    segments = lax.axis_size("segment")
    reach = min(4, (n - 1) // 2)
    flat = [x.reshape(patches, feature_width) for x in (queries, keys, values, out_grad)]
    weight = proj_weight[0]
    if n != 4:
        query_grad, pair, _ = attention_grads(*flat, links, reach, [lambda value: ()] * 3)
        grad_qkv = jnp.concatenate([query_grad, pair[0], pair[1]], axis=1)
        whole = lax.all_gather(weight, "var", axis=0, tiled=True)
        passed = passed_along(times(grad_qkv, whole), "segment", -1)
        return passed.reshape(1, 1, 1, patches, whole.shape[0])

    own = lax.axis_index("var")
    core = lax.axis_index("dp")
    chunk = weight.shape[0]
    cuts = [(0, CAUSAL_BLOCK), (CAUSAL_BLOCK, chunk)]
    step_near = [((v, 0), (v + 1, 0)) for v in range(3)] + [((v + 1, 1), (v, 1)) for v in range(3)]
    step_far = [((1, 0), (2, 0)), ((2, 0), (3, 0)), ((2, 1), (1, 1)), ((1, 1), (0, 1))]
    pieces = [weight[lo:hi] for lo, hi in cuts]
    near, swapped_near = [], []

    def send_first(value):
        pieces[:] = lax.optimization_barrier((*pieces, value))[:2]
        near.append(on_line(pieces[0], step_near))
        return near[:1]

    def send_second(value):
        near.append(on_line(after(pieces[1], value), step_near))

    def swap_near(value):
        swapped_near.extend(swapped(after(piece, value)) for piece in near)

    query_grad, pair, returned = attention_grads(
        *flat, links, reach, [send_first, send_second, swap_near]
    )
    inward = [(0, 1), (3, 2)]
    outer_pair = lax.ppermute(after(pair, returned[1]), "var", inward)
    outer_query = lax.ppermute(query_grad, "var", inward)
    far_here = (core == jnp.where(own < 2, 1, 0)).astype(jnp.int32).reshape(1)

    def handed_on(block, moves):
        route = [
            (a * segments + s, b * segments + (s - 1) % segments)
            for a, b in moves
            for s in range(segments)
        ]
        return lax.ppermute(block, ("var", "segment"), route)

    in_place = [(v, v) for v in range(4)]
    from_inner = [(1, 0), (2, 3)]
    own_set, outer_set = (query_grad, pair), (outer_query, outer_pair)
    (result,) = project(far_here, [own_set], [weight] + near + swapped_near)
    first = handed_on(result, in_place)
    joined = jnp.concatenate([near[1][chunk // 2 :], near[0]], axis=0)
    far = [
        on_line(after(rows, returned[1]), step_far) for rows in (near[1][: chunk // 2], joined)
    ]
    swapped_far = [
        swapped(after(far[0], result)),
        swapped(after(far[1], result, first, outer_pair, outer_query)),
    ]
    far_parts, end_parts = [], []
    for rows, others in zip(far, swapped_far):
        far_result, end = project(far_here, [own_set, outer_set], [rows], [others])
        far_parts.append(handed_on(far_result, in_place))
        end_parts.append(handed_on(end, from_inner))
    parts = far_parts + end_parts
    passed = pl.pallas_call(
        functools.partial(place_kernel, CAUSAL_BLOCK),
        in_specs=[pl.BlockSpec(memory_space=pltpu.VMEM)] * (1 + len(parts)),
        out_specs=pl.BlockSpec(memory_space=pltpu.VMEM),
        out_shape=jax.ShapeDtypeStruct((patches, 4 * chunk), bf16),
        name="placed",
    )(first, *parts)
    return passed.reshape(1, 1, 1, patches, 4 * chunk)


def solution(mesh):
    return jax.shard_map(
        shards,
        mesh=mesh,
        in_specs=(
            P("dp", "segment", "var", None, None),
            P("dp", "segment", "var", None, None),
            P("dp", "segment", "var", None, None),
            P("dp", "segment", "var", None, None),
            P("segment", "var", None),
            P(),
        ),
        out_specs=P("dp", "segment", "var", None, None),
        check_vma=False,
    )
```

```python
import functools
import math

import jax
import jax.numpy as jnp
from jax import lax
from jax.experimental import pallas as pl
from jax.experimental.pallas import tpu as pltpu
from jax.sharding import PartitionSpec as P

HEADS = 16
CAUSAL_BLOCK = 128
GROUP = 4

neg_big = -1e30
f32 = jnp.float32
bf16 = jnp.bfloat16


def passed_along(block, axis, distance):
    devices = range(lax.axis_size(axis))
    route = [((i - distance) % len(devices), i) for i in devices]
    return lax.ppermute(block, axis, route)


def spent(us):
    return pl.CostEstimate(flops=int(us * 1.15e9), bytes_accessed=1024, transcendentals=0)


def after(block, *earlier):
    return lax.optimization_barrier((block,) + earlier)[0]


def dot_nt(a, b):
    return lax.dot_general(a, b, (((1,), (1,)), ((), ())), preferred_element_type=f32)


def dot_nn(a, b):
    return lax.dot_general(a, b, (((1,), (0,)), ((), ())), preferred_element_type=f32)


def own_half(block, half, head_size):
    lane = lax.broadcasted_iota(jnp.int32, block.shape, 1)
    keep = (lane < head_size) if half == 0 else (lane >= head_size)
    return jnp.where(keep, block, jnp.zeros_like(block))


def block_products(key_half, value_half, query, grad, blocks):
    out = []
    for j in range(blocks):
        rows = slice(j * CAUSAL_BLOCK, (j + 1) * CAUSAL_BLOCK)
        start = j * CAUSAL_BLOCK
        out.append(
            (dot_nt(key_half[rows], query[start:]), dot_nt(value_half[rows], grad[start:]))
        )
    return out


def stats_kernel(sources, head_size, scale, linked_ref, k_ref, v_ref, *refs):
    ins, outs = refs[: 2 * sources], refs[2 * sources :]
    patches = k_ref.shape[0]
    blocks = patches // CAUSAL_BLOCK
    factor = scale * math.log2(math.e)
    for s in range(sources):
        linked = linked_ref[s] != 0
        lams, deltas = [], []
        for h in range(GROUP):
            cols = slice((h // 2) * 2 * head_size, (h // 2 + 1) * 2 * head_size)
            key_half = own_half(k_ref[:, cols], h % 2, head_size)
            value_half = own_half(v_ref[:, cols], h % 2, head_size)
            parts = block_products(
                key_half, value_half, ins[2 * s][:, cols], ins[2 * s + 1][:, cols], blocks
            )
            lam_row, delta_row = [], []
            for i in range(blocks):
                pieces = []
                for j in range(i + 1):
                    at = slice((i - j) * CAUSAL_BLOCK, (i - j + 1) * CAUSAL_BLOCK)
                    pieces.append((parts[j][0][:, at], parts[j][1][:, at]))
                top = functools.reduce(
                    jnp.maximum, [jnp.max(p[0], axis=0, keepdims=True) for p in pieces]
                )
                total = 0.0
                weighted = 0.0
                for score, grad_attn in pieces:
                    e = jnp.exp2((score - top) * factor)
                    total = total + jnp.sum(e, axis=0, keepdims=True)
                    weighted = weighted + jnp.sum(e * grad_attn, axis=0, keepdims=True)
                lam_row.append(top + jnp.log(total) * (1.0 / scale))
                delta_row.append(weighted / total)
            lams.append(jnp.concatenate(lam_row, axis=1))
            deltas.append(jnp.concatenate(delta_row, axis=1))
        lam = jnp.where(linked, jnp.concatenate(lams, axis=0), neg_big)
        delta = jnp.where(linked, jnp.concatenate(deltas, axis=0), 0.0)
        outs[s][0] = jnp.concatenate([lam, delta], axis=0)


def grads_kernel(sources, window, head_size, scale, linked_ref, k_ref, v_ref, *refs):
    ins = refs[: 2 * sources]
    stats = refs[2 * sources : 2 * sources + sources * window]
    outs = refs[2 * sources + sources * window :]
    own_out, part_outs, kv_out = outs[0], outs[1:sources], outs[sources]
    patches = k_ref.shape[0]
    blocks = patches // CAUSAL_BLOCK
    factor = scale * math.log2(math.e)
    key_t = jnp.transpose(k_ref[...].astype(f32)).astype(bf16)
    totals = []
    for s in range(sources):
        lams = [r[0, :GROUP] for r in stats[s * window : (s + 1) * window]]
        deltas = [r[0, GROUP:] for r in stats[s * window : (s + 1) * window]]
        top = functools.reduce(jnp.maximum, lams)
        weights = [jnp.exp2((lam - top) * factor) for lam in lams]
        total = functools.reduce(jnp.add, weights)
        delta = functools.reduce(jnp.add, [w * d for w, d in zip(weights, deltas)]) / total
        lam = top + jnp.log(total) * (1.0 / scale)
        lam = jnp.where(linked_ref[s] != 0, lam, -neg_big)
        totals.append((lam, delta))
    for pair in range(GROUP // 2):
        cols = slice(pair * 2 * head_size, (pair + 1) * 2 * head_size)
        halves = [
            (
                own_half(k_ref[:, cols], half, head_size),
                own_half(v_ref[:, cols], half, head_size),
            )
            for half in range(2)
        ]
        key_sum = jnp.zeros((patches, 2 * head_size), f32)
        value_sum = jnp.zeros((patches, 2 * head_size), f32)
        for s in range(sources):
            query, grad = ins[2 * s][:, cols], ins[2 * s + 1][:, cols]
            query_t = []
            for half in range(2):
                h = 2 * pair + half
                lam = totals[s][0][h : h + 1]
                delta = totals[s][1][h : h + 1]
                parts = block_products(*halves[half], query, grad, blocks)
                attn_rows, score_rows = [], []
                for j in range(blocks):
                    start = j * CAUSAL_BLOCK
                    attn = jnp.exp2((parts[j][0] - lam[:, start:]) * factor)
                    score_grad = (attn * (parts[j][1] - delta[:, start:])).astype(bf16)
                    attn = attn.astype(bf16)
                    if start:
                        pad = jnp.zeros((CAUSAL_BLOCK, start), bf16)
                        attn = jnp.concatenate([pad, attn], axis=1)
                        score_grad = jnp.concatenate([pad, score_grad], axis=1)
                    attn_rows.append(attn)
                    score_rows.append(score_grad)
                attn = jnp.concatenate(attn_rows, axis=0)
                score_grad = jnp.concatenate(score_rows, axis=0)
                key_sum = key_sum + dot_nn(score_grad, own_half(query, half, head_size))
                value_sum = value_sum + dot_nn(attn, own_half(grad, half, head_size))
                query_t.append(dot_nn(key_t[h * head_size : (h + 1) * head_size], score_grad))
            part = jnp.transpose(jnp.concatenate(query_t, axis=0)) * scale
            if s == 0:
                own_out[:, cols] = part
            else:
                part_outs[s - 1][:, cols] = part.astype(bf16)
        kv_out[0, :, cols] = (key_sum * scale).astype(bf16)
        kv_out[1, :, cols] = value_sum.astype(bf16)


def specs(patches, width):
    token = pl.BlockSpec((patches, width), lambda g: (0, g))
    stat = pl.BlockSpec((1, 2 * GROUP, patches), lambda g: (g, 0, 0))
    flag = pl.BlockSpec(memory_space=pltpu.SMEM)
    return token, stat, flag


def block_stats(linked, keys, values, pairs, head_size, scale):
    patches, features = keys.shape
    token, stat, flag = specs(patches, GROUP * head_size)
    groups = HEADS // GROUP
    n = len(pairs)
    return pl.pallas_call(
        functools.partial(stats_kernel, n, head_size, scale),
        grid=(groups,),
        in_specs=[flag] + [token] * (2 + 2 * n),
        out_specs=[stat] * n,
        out_shape=[jax.ShapeDtypeStruct((groups, 2 * GROUP, patches), f32)] * n,
        compiler_params=pltpu.CompilerParams(vmem_limit_bytes=48 * 2**20),
        cost_estimate=spent(0.025 * n),
        name="row_stats",
    )(linked, keys, values, *[x for pair in pairs for x in pair])


def block_grads(linked, keys, values, pairs, stats, head_size, scale):
    patches, features = keys.shape
    token, stat, flag = specs(patches, GROUP * head_size)
    groups = HEADS // GROUP
    n = len(pairs)
    window = len(stats[0])
    both = pl.BlockSpec((2, patches, GROUP * head_size), lambda g: (0, 0, g))
    shape = jax.ShapeDtypeStruct
    return pl.pallas_call(
        functools.partial(grads_kernel, n, window, head_size, scale),
        grid=(groups,),
        in_specs=[flag] + [token] * (2 + 2 * n) + [stat] * (n * window),
        out_specs=[token] * n + [both],
        out_shape=[shape((patches, features), f32)]
        + [shape((patches, features), bf16)] * (n - 1)
        + [shape((2, patches, features), bf16)],
        compiler_params=pltpu.CompilerParams(vmem_limit_bytes=48 * 2**20),
        cost_estimate=spent(48 * n),
        name="block_grads",
    )(
        linked,
        keys,
        values,
        *[x for pair in pairs for x in pair],
        *[x for group in stats for x in group],
    )


def place_kernel(roll, first_ref, *refs):
    far_refs, end_refs, out_ref = refs[:2], refs[2:4], refs[4]
    chunk = far_refs[0].shape[1] + far_refs[1].shape[1]
    own, core = lax.axis_index("var"), lax.axis_index("dp")
    is_end = (own == 0) | (own == 3)

    def put(ref, start, width, at, shift):
        col = pl.multiple_of(at * chunk + shift, CAUSAL_BLOCK)
        out_ref[:, pl.ds(col, width)] = ref[:, start : start + width]

    def put_rolled(pieces, at):
        shift = roll
        for ref in pieces:
            width = ref.shape[1]
            edge = min(width, chunk - shift)
            put(ref, 0, edge, at, shift)
            if edge < width:
                put(ref, edge, width - edge, at, 0)
            shift += width

    for i, at in enumerate(
        [own, lax.rem(own + 3 + 2 * core, 4), lax.rem(own + 1 + 2 * core, 4)]
    ):
        put(first_ref, i * chunk, chunk, at, 0)
    put_rolled(far_refs, lax.rem(own + 2, 4))
    pl.when(is_end)(lambda: put_rolled(end_refs, 3 - own))


def project_kernel(uses, sets, pieces, swaps, flag_ref, *refs):
    tokens, rows = refs[: 2 * sets], refs[2 * sets : 2 * sets + pieces * (1 + swaps)]
    outs = refs[2 * sets + pieces * (1 + swaps) :]
    features = tokens[0].shape[1]
    filled = [0] * sets

    def add(piece, cols):
        step = 256 if piece.shape[0] % 256 == 0 else CAUSAL_BLOCK

        @pl.loop(0, piece.shape[0] // step)
        def _(i):
            part = piece[pl.ds(pl.multiple_of(i * step, step), step), :]
            for t, col in cols:
                at = pl.ds(pl.multiple_of(col + i * step, CAUSAL_BLOCK), step)
                query, pair = tokens[2 * t], tokens[2 * t + 1]
                total = dot_nt(query[...], part[:, :features])
                total = total + dot_nt(pair[0], part[:, features : 2 * features])
                total = total + dot_nt(pair[1], part[:, 2 * features :])
                outs[t][:, at] = total.astype(bf16)

    for p in range(pieces):
        cols = [(t, filled[t]) for t in range(sets) if p in uses[t]]
        if swaps:
            pl.when(flag_ref[0] != 0)(functools.partial(add, rows[p], cols))
            pl.when(flag_ref[0] == 0)(functools.partial(add, rows[pieces + p], cols))
        else:
            add(rows[p], cols)
        for t, _ in cols:
            filled[t] += rows[p].shape[0]


def project(flag, token_sets, rows, other_rows=(), uses=None):
    patches = token_sets[0][0].shape[0]
    uses = uses or [list(range(len(rows)))] * len(token_sets)
    widths = [sum(rows[p].shape[0] for p in use) for use in uses]
    whole = pl.BlockSpec(memory_space=pltpu.VMEM)
    operands = [x for t in token_sets for x in t] + list(rows) + list(other_rows)
    return pl.pallas_call(
        functools.partial(
            project_kernel, uses, len(token_sets), len(rows), 1 if other_rows else 0
        ),
        in_specs=[pl.BlockSpec(memory_space=pltpu.SMEM)] + [whole] * len(operands),
        out_specs=[whole] * len(token_sets),
        out_shape=[jax.ShapeDtypeStruct((patches, width), bf16) for width in widths],
        compiler_params=pltpu.CompilerParams(vmem_limit_bytes=32 * 2**20),
        cost_estimate=spent(1 + 0.004 * sum(widths)),
        name="project",
    )(flag, *operands)


def times(tokens, rows):
    return dot_nt(tokens, rows).astype(bf16)


def swapped(block):
    return lax.ppermute(block, "dp", [(0, 1), (1, 0)])


def on_line(block, moves):
    return lax.ppermute(
        block, ("var", "dp"), [(a * 2 + c, b * 2 + d) for (a, c), (b, d) in moves]
    )


def attention_grads(queries, keys, values, out_grad, links, reach, sends):
    patches, feature_width = queries.shape
    head_size = feature_width // HEADS
    scale = 1.0 / math.sqrt(head_size)
    n = lax.axis_size("var")
    own = lax.axis_index("var")
    offsets = [0] + [o for d in range(1, reach + 1) for o in (d, -d)]
    pairs = [(queries, out_grad)]
    for o in offsets[1:]:
        pairs.append((passed_along(queries, "var", -o), passed_along(out_grad, "var", -o)))
    sources = (own + jnp.array(offsets, jnp.int32)) % n
    linked = jnp.any(links[sources] == own, axis=1).astype(jnp.int32)
    own_stats = block_stats(linked[:1], keys, values, pairs[:1], head_size, scale)
    first_sent = sends[0](own_stats[0])
    other_stats = block_stats(linked[1:], keys, values, pairs[1:], head_size, scale)
    stats = dict(zip(offsets, list(own_stats) + list(other_stats)))
    needed = {}
    for d in offsets:
        for e in offsets:
            entries = needed.setdefault((d + e) % n, [])
            if -e not in entries:
                entries.append(-e)
    arrived, messages = {}, []
    for t, entries in needed.items():
        if t == 0:
            arrived[t] = {o: stats[o] for o in entries}
            continue
        entries.sort()
        message = jnp.stack([stats[o] for o in entries])
        message = passed_along(message, "var", -t)
        messages.append(message)
        arrived[t] = {o: message[i] for i, o in enumerate(entries)}
    sends[1](messages[0])
    windows = [[arrived[(d + e) % n][-e] for e in offsets] for d in offsets]
    linked = after(linked, *first_sent)
    grads = block_grads(linked, keys, values, pairs, windows, head_size, scale)
    returned = [
        passed_along(part, "var", o) for o, part in zip(offsets[1:], grads[1:-1])
    ]
    sends[2](grads[-1])
    query_grad = grads[0]
    for part in returned:
        query_grad = query_grad + part.astype(f32)
    return query_grad.astype(bf16), grads[-1], returned


def shards(queries, keys, values, out_grad, proj_weight, links):
    patches, feature_width = queries.shape[3:]
    n = lax.axis_size("var")
    segments = lax.axis_size("segment")
    reach = min(4, (n - 1) // 2)
    flat = [x.reshape(patches, feature_width) for x in (queries, keys, values, out_grad)]
    weight = proj_weight[0]
    if n != 4:
        query_grad, pair, _ = attention_grads(*flat, links, reach, [lambda value: ()] * 3)
        grad_qkv = jnp.concatenate([query_grad, pair[0], pair[1]], axis=1)
        whole = lax.all_gather(weight, "var", axis=0, tiled=True)
        passed = passed_along(times(grad_qkv, whole), "segment", -1)
        return passed.reshape(1, 1, 1, patches, whole.shape[0])

    own = lax.axis_index("var")
    core = lax.axis_index("dp")
    chunk = weight.shape[0]
    cuts = [(0, CAUSAL_BLOCK), (CAUSAL_BLOCK, chunk)]
    step_near = [((v, 0), (v + 1, 0)) for v in range(3)] + [((v + 1, 1), (v, 1)) for v in range(3)]
    step_far = [((1, 0), (2, 0)), ((2, 0), (3, 0)), ((2, 1), (1, 1)), ((1, 1), (0, 1))]
    pieces = [weight[lo:hi] for lo, hi in cuts]
    near, swapped_near = [], []

    def send_first(value):
        pieces[:] = lax.optimization_barrier((*pieces, value))[:2]
        near.append(on_line(pieces[0], step_near))
        return near[:1]

    def send_second(value):
        near.append(on_line(after(pieces[1], value), step_near))

    def swap_near(value):
        swapped_near.extend(swapped(after(piece, value)) for piece in near)

    query_grad, pair, returned = attention_grads(
        *flat, links, reach, [send_first, send_second, swap_near]
    )
    inward = [(0, 1), (3, 2)]
    outer_pair = lax.ppermute(after(pair, returned[1]), "var", inward)
    outer_query = lax.ppermute(query_grad, "var", inward)
    far_here = (core == jnp.where(own < 2, 1, 0)).astype(jnp.int32).reshape(1)

    def handed_on(block, moves):
        route = [
            (a * segments + s, b * segments + (s - 1) % segments)
            for a, b in moves
            for s in range(segments)
        ]
        return lax.ppermute(block, ("var", "segment"), route)

    in_place = [(v, v) for v in range(4)]
    from_inner = [(1, 0), (2, 3)]
    own_set, outer_set = (query_grad, pair), (outer_query, outer_pair)
    (result,) = project(far_here, [own_set], [weight] + near + swapped_near)
    first = handed_on(result, in_place)
    joined = jnp.concatenate([near[1][chunk // 2 :], near[0]], axis=0)
    far = [
        on_line(after(rows, returned[1]), step_far) for rows in (near[1][: chunk // 2], joined)
    ]
    swapped_far = [
        swapped(after(far[0], result)),
        swapped(after(far[1], result, first, outer_pair, outer_query)),
    ]
    far_parts, end_parts = [], []
    for rows, others in zip(far, swapped_far):
        far_result, end = project(far_here, [own_set, outer_set], [rows], [others])
        far_parts.append(handed_on(far_result, in_place))
        end_parts.append(handed_on(end, from_inner))
    parts = far_parts + end_parts
    passed = pl.pallas_call(
        functools.partial(place_kernel, CAUSAL_BLOCK),
        in_specs=[pl.BlockSpec(memory_space=pltpu.VMEM)] * (1 + len(parts)),
        out_specs=pl.BlockSpec(memory_space=pltpu.VMEM),
        out_shape=jax.ShapeDtypeStruct((patches, 4 * chunk), bf16),
        name="placed",
    )(first, *parts)
    return passed.reshape(1, 1, 1, patches, 4 * chunk)


def solution(mesh):
    return jax.shard_map(
        shards,
        mesh=mesh,
        in_specs=(
            P("dp", "segment", "var", None, None),
            P("dp", "segment", "var", None, None),
            P("dp", "segment", "var", None, None),
            P("dp", "segment", "var", None, None),
            P("segment", "var", None),
            P(),
        ),
        out_specs=P("dp", "segment", "var", None, None),
        check_vma=False,
    )
```
